256 devices in a mesh: dp: 16 (over x, y), expert: 16 (over z, core).
Axes of the slice: x: 4, y: 4, z: 8, core: 2. Of those that a mesh axis runs over, the one named last changes fastest.
Arguments:
- tokens: bfloat16 [32768, 1024], P(('dp', 'expert')), may hold values from -6 to 6
- out_grad: bfloat16 [32768, 1024], P(('dp', 'expert')), may hold values from -6 to 6
- expert_ids: int32 [32768, 8], P(('dp', 'expert')), may hold values from 0 to 63, all different within a row; in each aligned block of 128 rows (0 to 127, 128 to 255, ...) at most 24 rows name the same one
- gates: float32 [32768, 8], P(('dp', 'expert')), may hold values from 0.05 to 0.5
- w_gate_up: bfloat16 [64, 1024, 768], P('expert'), may hold values from -0.1875 to 0.1875
- w_down: bfloat16 [64, 384, 1024], P('expert'), may hold values from -0.3125 to 0.3125
Outputs:
- in_grad: bfloat16 [32768, 1024], P(('dp', 'expert'))
- grad_gate_up: float32 [1024, 64, 768], P('dp', 'expert')
- grad_down: float32 [384, 64, 1024], P('dp', 'expert')
The draws below stay inside these ranges and needn't reach their ends.
Inputs may be any that keep to these rules, and one draw needn't show every extreme that they name: `expert_ids`: among the rows of one device no expert is named more than 24 times, and this bound is reached; each row names 8 different experts.
All inputs are finite; a program needn't handle non-finite values.
Results may differ from the reference program's by a relative error of at most 0.015.
Values may be sent and summed in bfloat16 or wider, within the bound.
No kernel may reach another device: no remote copies, remote signals or barrier semaphores. Data moves between devices by JAX's collectives and lax.ppermute only.
A program may use at most 128 MiB of HBM per device.

```python
import math
import jax
import jax.numpy as jnp
import numpy as np
from jax import lax

D = 1024
FF = 384
TOP = 8
TOK_DEV = 128
EXPERTS = 64
CAP = 24
TOKENS = 32768
N_DP = 16
N_EXPERT = 16


def level_of(own_key, extent, shards, low, largest):
    loudness, own = 1.0, jax.random.fold_in(own_key, 6)
    for position, parts in shards:
        heights = jnp.exp(jax.random.uniform(jax.random.fold_in(own, position), (parts,), jnp.float32, low / len(shards), largest / len(shards)))
        loudness = loudness * jnp.repeat(heights, extent[position] // parts).reshape([-1 if axis == position else 1 for axis in range(len(extent))])
    return loudness


def deal_out(key, own, number, rows, count, top, most, slope):
    order = jax.random.permutation(key, count)
    heavy_load, ordinary = portions_of(count, rows * top, most, slope, True), portions_of(count, rows * top, most, slope, False)
    places = jnp.arange(count)

    def named(sizes, offset_by):
        used = int((sizes > 0).sum())
        fixed = max(1, used // 4)
        moved = fixed + (places - fixed + offset_by * (used - fixed)) % max(1, count - fixed)
        return jnp.zeros((count,), jnp.int32).at[order[jnp.where(places < fixed, places, moved)]].set(jnp.asarray(sizes, jnp.int32))

    sizes = jnp.where(number % 4 == 0, named(heavy_load, number // 4), named(ordinary, number - number // 4 - 1))
    mixed = jax.random.permutation(jax.random.fold_in(own, 3), count)
    giver, receiver = mixed[0:count // 2 * 2:2], mixed[1:count // 2 * 2:2]
    slack = jnp.minimum(sizes[giver] - 1, most - sizes[receiver]) // 2
    slack = jnp.where((giver == order[0]) | (receiver == order[0]) | (sizes[receiver] == 0), 0, jnp.maximum(slack, 0))
    moved = jax.random.randint(jax.random.fold_in(own, 4), (count // 2,), 0, 1 << 20) % (slack + 1)
    sizes = sizes.at[giver].add(-moved).at[receiver].add(moved)
    labels = jnp.searchsorted(jnp.cumsum(sizes), jnp.arange(rows * top), side="right").astype(jnp.int32)
    table = labels.reshape(top, rows).T
    table = table[jax.random.permutation(jax.random.fold_in(own, 1), rows)]
    offset_by = jax.random.randint(jax.random.fold_in(own, 2), (rows, 1), 0, top)
    return jnp.take_along_axis(table, (jnp.arange(top)[None, :] + offset_by) % top, axis=1)


def portions_of(amount, total, reach, lean, full):
    weights = [(1 << 20) // math.isqrt(grade ** lean) + 1 for grade in range(1, amount + 1)]
    largest = reach if full else min(reach, max(-(-total // amount), total * weights[0] // sum(weights)))
    least = 1 if total - largest >= amount - 1 else 0
    given, spare = [largest] + [least] * (amount - 1), total - largest - least * (amount - 1)
    while spare > 0:
        candidates = [i for i in range(1, amount) if given[i] < largest] or [i for i in range(1, amount) if given[i] < reach]
        mass, remaining = sum([weights[i] for i in candidates]), spare
        for i in candidates:
            more = min(reach - given[i], max(1, remaining * weights[i] // mass), spare)
            given[i] = given[i] + more
            spare = spare - more
    return np.array(given)


def centred(rng, extent, scale, reach, split=(), kind=jnp.bfloat16):
    factor_of = level_of(rng, extent, split, -0.22, 0.18) if split else 1.0
    entries = jax.random.normal(rng, extent, jnp.float32) * scale * factor_of
    return jnp.minimum(jnp.maximum(entries, -reach), reach).astype(kind)


def setup_inputs(seed: int = 0) -> dict:
    keys = jax.random.split(jax.random.key(seed), 7)
    tokens = centred(keys[0], (TOKENS, D), 1.0, 6.0, ((0, 256),))
    out_grad = centred(keys[1], (TOKENS, D), 1.0, 6.0, ((0, 256),))
    expert_ids_keys = jax.random.split(jax.random.fold_in(keys[2], 1), TOKENS // TOK_DEV)
    expert_ids_turns = jax.random.permutation(jax.random.fold_in(keys[2], 3), TOKENS // TOK_DEV)
    expert_ids = jax.vmap(lambda own, number: deal_out(jax.random.fold_in(keys[2], 2), own, number, TOK_DEV, EXPERTS, TOP, CAP, 2))(expert_ids_keys, expert_ids_turns).reshape((TOKENS, TOP))
    gates = jnp.clip(jnp.exp(math.log(0.5) - 2.3025851 * jax.random.uniform(keys[3], (TOKENS, TOP), jnp.float32) ** level_of(keys[3], (TOKENS, TOP), ((0, 256),), -0.2, 0.2)), 0.05, 0.5)
    w_gate_up = centred(keys[4], (EXPERTS, D, 2 * FF), D ** -0.5, 0.1875, ((0, 16),))
    w_down = centred(keys[5], (EXPERTS, FF, D), FF ** -0.5, 0.3125, ((0, 16),))
    return {"tokens": tokens, "out_grad": out_grad, "expert_ids": expert_ids, "gates": gates, "w_gate_up": w_gate_up, "w_down": w_down}


def reference(tokens, out_grad, expert_ids, gates, w_gate_up, w_down):
    devices = N_DP * N_EXPERT
    routes_dev = TOK_DEV * TOP
    empty_id = TOKENS * TOP
    flat = expert_ids.reshape(devices, routes_dev)
    onehot = (flat[:, :, None] == jnp.arange(EXPERTS, dtype=jnp.int32)[None, None, :]).astype(jnp.int32)
    earlier = jnp.cumsum(onehot, axis=1) - onehot
    slot = jnp.sum(earlier * onehot, axis=2).astype(jnp.int32)
    target = (flat * CAP + slot).astype(jnp.int32)
    route_id = jnp.arange(devices * routes_dev, dtype=jnp.int32).reshape(devices, routes_dev)
    owner_row = jnp.arange(devices, dtype=jnp.int32)[:, None] * jnp.ones_like(target)
    table = jnp.full((devices, EXPERTS * CAP), empty_id, jnp.int32).at[owner_row, target].set(route_id)
    table = table.reshape(N_DP, N_EXPERT, EXPERTS, CAP).transpose(2, 0, 1, 3).reshape(EXPERTS, N_DP, N_EXPERT * CAP)
    gate_flat = gates.reshape(-1)
    highest = lax.Precision.HIGHEST

    def one_expert(acc, pieces):
        routes, wgu, wdn = pieces
        valid = routes < empty_id
        safe = jnp.where(valid, routes, 0)
        tok = safe // TOP
        x_rows = jnp.where(valid[..., None], tokens[tok], jnp.zeros((), jnp.bfloat16))
        s_rows = jnp.where(valid[..., None], gate_flat[safe][..., None] * out_grad[tok].astype(jnp.float32), 0.0).astype(jnp.bfloat16)
        xf = x_rows.astype(jnp.float32)
        sf = s_rows.astype(jnp.float32)
        wguf = wgu.astype(jnp.float32)
        wdnf = wdn.astype(jnp.float32)
        both = jnp.einsum("grd,df->grf", xf, wguf, precision=highest)
        gate_pre = both[..., :FF]
        up_val = both[..., FF:]
        sig = jax.nn.sigmoid(gate_pre)
        act = gate_pre * sig
        hidden = (act * up_val).astype(jnp.bfloat16)
        dh = jnp.einsum("grd,fd->grf", sf, wdnf, precision=highest)
        d_gate = dh * up_val * sig * (1.0 + gate_pre * (1.0 - sig))
        d_up = dh * act
        d_both = jnp.concatenate([d_gate, d_up], axis=-1).astype(jnp.bfloat16)
        dbf = d_both.astype(jnp.float32)
        route_grad = jnp.einsum("grf,df->grd", dbf, wguf, precision=highest).astype(jnp.bfloat16)
        tok_target = jnp.where(valid, tok, TOKENS).reshape(-1)
        acc = acc.at[tok_target].add(route_grad.reshape(-1, D).astype(jnp.float32), mode="drop")
        part_gu = jnp.einsum("grd,grf->gdf", xf, dbf, precision=highest)
        part_gu = lax.optimization_barrier(part_gu.astype(jnp.bfloat16)).astype(jnp.float32)
        part_dn = jnp.einsum("grf,grd->gfd", hidden.astype(jnp.float32), sf, precision=highest)
        part_dn = lax.optimization_barrier(part_dn.astype(jnp.bfloat16)).astype(jnp.float32)
        return acc, (jnp.sum(part_gu, axis=0), jnp.sum(part_dn, axis=0))

    start = jnp.zeros((TOKENS, D), jnp.float32)
    acc, (grad_gu, grad_dn) = lax.scan(one_expert, start, (table, w_gate_up, w_down))
    return acc.astype(jnp.bfloat16), grad_gu.transpose(1, 0, 2), grad_dn.transpose(1, 0, 2)
```

```python
import functools

import jax
import jax.numpy as jnp
from jax import lax
from jax.experimental import pallas as pl
from jax.experimental.pallas import tpu as pltpu
from jax.sharding import PartitionSpec as P

TOK = 128
TOP = 8
D = 1024
FF = 384
CAP = 24
EXP = 4
OWN = 16
SIDE = 4
GU_ROWS = D // 16
DN_ROWS = FF // 16
PAIR = 2 * CAP
ROWS = OWN * CAP
BLK = 2 * (3 * GU_ROWS // 4 + DN_ROWS)
CUT = 80
BF = jnp.bfloat16
F32 = jnp.float32
MB = 1 << 20


def dot(a, b, dims):
    return lax.dot_general(a, b, (dims, ((), ())), preferred_element_type=F32)


NN = ((1,), (0,))
NT = ((1,), (1,))
TN = ((0,), (0,))


def vmem(limit):
    return pltpu.CompilerParams(vmem_limit_bytes=limit * MB)


def prep_kernel(x_ref, g_ref, ids_ref, gates_ref, out_ref):
    out_ref[:, :D] = x_ref[...]
    out_ref[:, D : 2 * D] = g_ref[...]
    gate = gates_ref[...]
    high = gate.astype(BF)
    rest = gate - high.astype(F32)
    mid = rest.astype(BF)
    low = (rest - mid.astype(F32)).astype(BF)
    out_ref[:, 2 * D :] = jnp.zeros((TOK, 128), BF)
    top = jnp.concatenate([ids_ref[...].astype(F32).astype(BF), high], axis=0)
    out_ref[0:16, 2 * D :] = top
    out_ref[16:32, 2 * D :] = jnp.concatenate([mid, low], axis=0)


def prep(tokens, out_grad, ids_t, gates_t):
    return pl.pallas_call(
        prep_kernel,
        out_shape=jax.ShapeDtypeStruct((TOK, 2 * D + 128), BF),
        cost_estimate=pl.CostEstimate(flops=0, bytes_accessed=MB, transcendentals=0),
    )(tokens, out_grad, ids_t, gates_t)


def route_kernel(q_ref, pay_ref, x_ref, s_ref, oh_ref):
    first = (q_ref[0] * EXP).astype(F32)
    before = (
        lax.broadcasted_iota(jnp.int32, (TOK, TOK), 0)
        < lax.broadcasted_iota(jnp.int32, (TOK, TOK), 1)
    ).astype(BF)
    named, gate = [], []
    for i in range(2):
        meta_a = pay_ref[i, 0:16, 2 * D :].astype(F32)
        meta_b = pay_ref[i, 16:32, 2 * D :].astype(F32)
        ids = meta_a[0:TOP]
        gates = (meta_a[TOP:] + meta_b[0:TOP]) + meta_b[TOP:]
        for j in range(EXP):
            hit = ids == first + float(j)
            named.append(jnp.sum(jnp.where(hit, 1.0, 0.0), axis=0, keepdims=True))
            gate.append(jnp.sum(jnp.where(hit, gates, 0.0), axis=0, keepdims=True))
    mask = jnp.concatenate(named, axis=0)
    rank = dot(mask.astype(BF), before, NN)
    target = jnp.where(mask > 0.5, rank, -1000.0)
    row = lax.broadcasted_iota(jnp.int32, (PAIR, 2 * TOK), 0).astype(F32)
    picks, weights = [], []
    for j in range(EXP):
        place = jnp.concatenate([target[j : j + 1], target[EXP + j : EXP + j + 1] + float(CAP)], axis=1)
        gates = jnp.concatenate([gate[j], gate[EXP + j]], axis=1)
        hit = row == place
        picks.append(jnp.where(hit, 1.0, 0.0))
        weights.append(jnp.sum(jnp.where(hit, gates, 0.0), axis=1, keepdims=True))
    pick = jnp.concatenate(picks, axis=0).astype(BF)
    weight = jnp.concatenate(weights, axis=0)
    oh_ref[0] = pick
    x = pay_ref[:, :, :D].reshape(2 * TOK, D)
    g = pay_ref[:, :, D : 2 * D].reshape(2 * TOK, D)
    x_rows = dot(pick, x, NN).astype(BF)
    s_rows = (dot(pick, g, NN) * weight).astype(BF)
    for j in range(EXP):
        x_ref[j] = x_rows[j * PAIR : (j + 1) * PAIR]
        s_ref[j] = s_rows[j * PAIR : (j + 1) * PAIR]


def route(q, pay):
    pairs = OWN // 2
    rows = jax.ShapeDtypeStruct((EXP, ROWS, D), BF)
    spec = pl.BlockSpec((EXP, PAIR, D), lambda i, q: (0, i, 0))
    return pl.pallas_call(
        route_kernel,
        out_shape=(rows, rows, jax.ShapeDtypeStruct((pairs, EXP * PAIR, 2 * TOK), BF)),
        grid_spec=pltpu.PrefetchScalarGridSpec(
            num_scalar_prefetch=1,
            grid=(pairs,),
            in_specs=[pl.BlockSpec((2, TOK, 2 * D + 128), lambda i, q: (i, 0, 0))],
            out_specs=(spec, spec, pl.BlockSpec((1, EXP * PAIR, 2 * TOK), lambda i, q: (i, 0, 0))),
        ),
        compiler_params=vmem(32),
        cost_estimate=pl.CostEstimate(flops=2 * 2 * 1536 * 256 * D, bytes_accessed=15 * MB, transcendentals=0),
    )(q, pay)


def grads_kernel(where_ref, x_ref, s_ref, wgu_ref, wdn_ref, o0, o1, o3, o2a, o2b, d_ref, pgu, pdn):
    jj = pl.program_id(0)
    x, s = x_ref[0], s_ref[0]
    both = dot(x, wgu_ref[0], NN)
    gate_pre, up_val = both[:, :FF], both[:, FF:]
    sig = jax.nn.sigmoid(gate_pre)
    act = gate_pre * sig
    hidden = (act * up_val).astype(BF)
    dh = dot(s, wdn_ref[0], NT)
    d_gate = dh * up_val * sig * (1.0 + gate_pre * (1.0 - sig))
    d_both = jnp.concatenate([d_gate, dh * act], axis=1).astype(BF)
    d_ref[0] = d_both
    pgu[...] = dot(x, d_both, TN)
    pdn[jj] = dot(hidden, s, TN)

    def outs():
        for first in range(SIDE):
            for second in range(SIDE):
                if first == 2:
                    ref, at = (o2a, second) if second < 2 else (o2b, second - 2)
                else:
                    ref, at = {0: o0, 1: o1, 3: o3}[first], second
                yield first * SIDE + second, ref, at

    for step in range(2):

        @pl.when(jj == step)
        def _():
            for number, ref, at in outs():
                base = pl.multiple_of(where_ref[number] * GU_ROWS, GU_ROWS)
                for a in range(4):
                    for b in range(3):
                        n = a * 3 + b
                        ref[at, 48 * step + 16 * (n // 4) : 48 * step + 16 * (n // 4) + 16, 256 * (n % 4) : 256 * (n % 4) + 256] = pgu[pl.ds(base + 16 * a, 16), 256 * b : 256 * b + 256].astype(BF)
                if step == 1:
                    low = pl.multiple_of(where_ref[number] * DN_ROWS, DN_ROWS)
                    ref[at, 96:BLK, :] = jnp.concatenate([pdn[0, pl.ds(low, DN_ROWS), :], pdn[1, pl.ds(low, DN_ROWS), :]], axis=0).astype(BF)


def grads(half, where, x_rows, s_rows, w_gate_up, w_down):
    def at(j, w):
        return (2 * half + j, 0, 0)

    def whole(j, w):
        return (0, 0, 0)

    def shape(n):
        return jax.ShapeDtypeStruct((n, BLK, D), BF)

    counts = (4, 4, 4, 2, 2)
    return pl.pallas_call(
        grads_kernel,
        out_shape=tuple(shape(n) for n in counts) + (jax.ShapeDtypeStruct((2, ROWS, 2 * FF), BF),),
        grid_spec=pltpu.PrefetchScalarGridSpec(
            num_scalar_prefetch=1,
            grid=(2,),
            in_specs=[
                pl.BlockSpec((1, ROWS, D), at),
                pl.BlockSpec((1, ROWS, D), at),
                pl.BlockSpec((1, D, 2 * FF), at),
                pl.BlockSpec((1, FF, D), at),
            ],
            out_specs=tuple(pl.BlockSpec((n, BLK, D), whole) for n in counts) + (pl.BlockSpec((1, ROWS, 2 * FF), lambda j, w: (j, 0, 0)),),
            scratch_shapes=[pltpu.VMEM((D, 2 * FF), F32), pltpu.VMEM((2, FF, D), F32)],
        ),
        compiler_params=vmem(48),
        cost_estimate=pl.CostEstimate(flops=2 * 2 * ROWS * D * FF * 6, bytes_accessed=12 * MB, transcendentals=0),
    )(where, x_rows, s_rows, w_gate_up, w_down)


def back_kernel(da_ref, db_ref, wgu_ref, oh_ref, out_ref, rg):
    j = pl.program_id(0)

    @pl.when(j < 2)
    def _():
        rg[j] = dot(da_ref[0], wgu_ref[0], NT).astype(BF)

    @pl.when(j >= 2)
    def _():
        rg[j] = dot(db_ref[0], wgu_ref[0], NT).astype(BF)

    @pl.when(j == EXP - 1)
    def _():
        for i in range(OWN // 2):
            rows = jnp.concatenate([rg[n, i * PAIR : (i + 1) * PAIR, :] for n in range(EXP)], axis=0)
            out_ref[2 * i * TOK : 2 * (i + 1) * TOK, :] = dot(oh_ref[i], rows, TN).astype(BF)


def back(d_a, d_b, w_gate_up, oh):
    return pl.pallas_call(
        back_kernel,
        out_shape=jax.ShapeDtypeStruct((OWN * TOK, D), BF),
        grid=(EXP,),
        in_specs=[
            pl.BlockSpec((1, ROWS, 2 * FF), lambda j: (jnp.minimum(j, 1), 0, 0)),
            pl.BlockSpec((1, ROWS, 2 * FF), lambda j: (jnp.maximum(j - 2, 0), 0, 0)),
            pl.BlockSpec((1, D, 2 * FF), lambda j: (j, 0, 0)),
            pl.BlockSpec((OWN // 2, EXP * PAIR, 2 * TOK), lambda j: (0, 0, 0)),
        ],
        out_specs=pl.BlockSpec((OWN * TOK, D), lambda j: (0, 0)),
        scratch_shapes=[pltpu.VMEM((EXP, ROWS, D), BF)],
        compiler_params=vmem(40),
        cost_estimate=pl.CostEstimate(flops=2 * 1536 * D * (2 * FF + 256), bytes_accessed=16 * MB, transcendentals=0),
    )(d_a, d_b, w_gate_up, oh)


def add1_kernel(o1, ra, o3, rb, s1, s3):
    s1[0:2] = (o1[0:2].astype(F32) + ra[...].astype(F32)).astype(BF)
    s1[2:4] = o1[2:4]
    s3[0:2] = o3[0:2]
    s3[2:4] = (o3[2:4].astype(F32) + rb[...].astype(F32)).astype(BF)


def add1(o1, ra, o3, rb):
    out = jax.ShapeDtypeStruct((SIDE, BLK, D), BF)
    return pl.pallas_call(
        add1_kernel,
        out_shape=(out, out),
        compiler_params=vmem(32),
        cost_estimate=pl.CostEstimate(flops=0, bytes_accessed=6 * MB, transcendentals=0),
    )(o1, ra, o3, rb)


def add2_kernel(o0, r1, r3, f0, f1, f3, f2a, f2b):
    def total(k):
        return (o0[k].astype(F32) + r1[k].astype(F32)) + r3[k].astype(F32)

    f0[...] = total(0)
    f1[...] = total(1).astype(BF)
    f3[...] = total(3).astype(BF)
    two = total(2).astype(BF)
    f2a[...] = two[:CUT]
    f2b[...] = two[CUT:]


def add2(o0, r1, r3):
    whole = jax.ShapeDtypeStruct((BLK, D), BF)
    return pl.pallas_call(
        add2_kernel,
        out_shape=(
            jax.ShapeDtypeStruct((BLK, D), F32),
            whole,
            whole,
            jax.ShapeDtypeStruct((CUT, D), BF),
            jax.ShapeDtypeStruct((BLK - CUT, D), BF),
        ),
        compiler_params=vmem(32),
        cost_estimate=pl.CostEstimate(flops=0, bytes_accessed=5 * MB, transcendentals=0),
    )(o0, r1, r3)


def add3_kernel(f1, ra, f3, rb, s1, s3):
    s1[:CUT] = (f1[:CUT].astype(F32) + ra[...].astype(F32)).astype(BF)
    s1[CUT:] = f1[CUT:]
    s3[:CUT] = f3[:CUT]
    s3[CUT:] = (f3[CUT:].astype(F32) + rb[...].astype(F32)).astype(BF)


def add3(f1, ra, f3, rb):
    out = jax.ShapeDtypeStruct((BLK, D), BF)
    return pl.pallas_call(
        add3_kernel,
        out_shape=(out, out),
        cost_estimate=pl.CostEstimate(flops=0, bytes_accessed=MB, transcendentals=0),
    )(f1, ra, f3, rb)


def last_kernel(a0, a1, a3, b0, b1, b3, gu_ref, dn_ref):
    for half, (f0, r1, r3) in enumerate(((a0, a1, a3), (b0, b1, b3))):
        total = f0[...] + r1[...].astype(F32) + r3[...].astype(F32)
        for e in range(2):
            for a in range(4):
                for b in range(3):
                    n = a * 3 + b
                    gu_ref[16 * a : 16 * a + 16, 2 * FF * (2 * half + e) + 256 * b : 2 * FF * (2 * half + e) + 256 * b + 256] = total[48 * e + 16 * (n // 4) : 48 * e + 16 * (n // 4) + 16, 256 * (n % 4) : 256 * (n % 4) + 256]
            dn_ref[:, D * (2 * half + e) : D * (2 * half + e + 1)] = total[96 + DN_ROWS * e : 96 + DN_ROWS * (e + 1), :]


def last(*pieces):
    return pl.pallas_call(
        last_kernel,
        out_shape=(
            jax.ShapeDtypeStruct((GU_ROWS, EXP * 2 * FF), F32),
            jax.ShapeDtypeStruct((DN_ROWS, EXP * D), F32),
        ),
        compiler_params=vmem(32),
        cost_estimate=pl.CostEstimate(flops=0, bytes_accessed=4 * MB, transcendentals=0),
    )(*pieces)


def along(axis, step):
    pairs = []
    for i in range(SIDE * SIDE):
        x, y = divmod(i, SIDE)
        x, y = ((x + step) % SIDE, y) if axis == 0 else (x, (y + step) % SIDE)
        pairs.append((i, x * SIDE + y))
    return pairs


def move(block, axis, step):
    return lax.ppermute(block, "dp", along(axis, step))


def stage_one(axis, o0, o1, o3, o2a, o2b):
    ra, rb = move(o2a, axis, 1), move(o2b, axis, -1)
    s1, s3 = add1(o1, ra, o3, rb)
    r1, r3 = move(s1, axis, 1), move(s3, axis, -1)
    return add2(o0, r1, r3)


def stage_two(axis, f0, f1, f3, f2a, f2b):
    ra, rb = move(f2a, axis, 1), move(f2b, axis, -1)
    s1, s3 = add3(f1, ra, f3, rb)
    return f0, move(s1, axis, 1), move(s3, axis, -1)


def per_device(tokens, out_grad, expert_ids, gates, w_gate_up, w_down):
    p, q = lax.axis_index("dp"), lax.axis_index("expert")
    px, py = p // SIDE, p % SIDE
    near = jnp.arange(SIDE, dtype=jnp.int32)
    xs, ys = (px + near) % SIDE, (py + near) % SIDE
    where_a = (xs[:, None] * SIDE + ys[None, :]).reshape(-1).astype(jnp.int32)
    where_b = (xs[None, :] * SIDE + ys[:, None]).reshape(-1).astype(jnp.int32)
    pay = lax.all_gather(prep(tokens, out_grad, expert_ids.T, gates.T), "expert")
    x_rows, s_rows, oh = route(q.reshape(1).astype(jnp.int32), pay)
    *blocks_a, d_a = grads(0, where_a, x_rows, s_rows, w_gate_up, w_down)
    *blocks_b, d_b = grads(1, where_b, x_rows, s_rows, w_gate_up, w_down)
    partial = back(d_a, d_b, w_gate_up, oh)
    in_grad = lax.psum_scatter(partial, "expert", scatter_dimension=0, tiled=True)
    a = stage_two(1, *stage_one(0, *blocks_a))
    b = stage_two(0, *stage_one(1, *blocks_b))
    gu, dn = last(*a, *b)
    return in_grad, gu.reshape(GU_ROWS, EXP, 2 * FF), dn.reshape(DN_ROWS, EXP, D)


def solution(mesh):
    spec = P(("dp", "expert"), None)
    return jax.shard_map(
        per_device,
        mesh=mesh,
        in_specs=(spec, spec, spec, spec, P("expert", None, None), P("expert", None, None)),
        out_specs=(spec, P("dp", "expert", None), P("dp", "expert", None)),
        check_vma=False,
    )
```

```python
import functools

import jax
import jax.numpy as jnp
from jax import lax
from jax.experimental import pallas as pl
from jax.experimental.pallas import tpu as pltpu
from jax.sharding import PartitionSpec as P

TOK = 128
TOP = 8
D = 1024
FF = 384
CAP = 24
EXP = 4
OWN = 16
LINE = 8
SIDE = 4
GU_ROWS = D // 16
DN_ROWS = FF // 16
PAIR = 2 * CAP
ROWS = OWN * CAP
BLK = 2 * (3 * GU_ROWS // 4 + DN_ROWS)
CUT = 80
LANES = 128
PARTS = D // LANES
PAY = 2 * PARTS + 1
BF = jnp.bfloat16
F32 = jnp.float32
MB = 1 << 20


def dot(a, b, dims):
    return lax.dot_general(a, b, (dims, ((), ())), preferred_element_type=F32)


NN = ((1,), (0,))
NT = ((1,), (1,))
TN = ((0,), (0,))


def ask(limit):
    return pltpu.CompilerParams(vmem_limit_bytes=limit * MB)


def prep_kernel(me_ref, x_ref, g_ref, ids_ref, gates_ref, out_ref):
    for i in range(PARTS):
        out_ref[i] = x_ref[:, i * LANES : (i + 1) * LANES]
        out_ref[PARTS + i] = g_ref[:, i * LANES : (i + 1) * LANES]
    gate = gates_ref[...]
    high = gate.astype(BF)
    rest = gate - high.astype(F32)
    mid = rest.astype(BF)
    low = (rest - mid.astype(F32)).astype(BF)
    out_ref[2 * PARTS] = jnp.zeros((TOK, LANES), BF)
    out_ref[2 * PARTS, 0:16] = jnp.concatenate([ids_ref[...].astype(F32).astype(BF), high], axis=0)
    out_ref[2 * PARTS, 16:32] = jnp.concatenate([mid, low], axis=0)


def prep(me, tokens, out_grad, ids_t, gates_t):
    return pl.pallas_call(
        prep_kernel,
        out_shape=jax.ShapeDtypeStruct((PAY, TOK, LANES), BF),
        in_specs=[pl.BlockSpec(memory_space=pltpu.SMEM)] + [pl.BlockSpec(memory_space=pltpu.VMEM)] * 4,
        compiler_params=ask(58),
        name="prep",
        cost_estimate=pl.CostEstimate(flops=0, bytes_accessed=MB, transcendentals=0),
    )(me, tokens, out_grad, ids_t, gates_t)


def owner(q, step, other):
    return 2 * (((q >> 1) + step) & (LINE - 1)) + ((q + other) & 1)


def work_kernel(pairs, split, done, steps, me_ref, *refs):
    count = 4 if split else 2 * pairs
    pays, refs = refs[:count], refs[count:]
    wgu_ref, wdn_ref = refs[:2]
    earlier, refs = refs[2 : 2 + len(done)], refs[2 + len(done) :]
    x_out, s_out, d_out, h_out, sums_out, xs, ss, rg, oh, stage, sems = refs
    last = bool(done)
    moves, place = [], 0
    if last:
        q = me_ref[1]
        for ref, n in [*zip(earlier, done), (stage, pairs)]:
            for k in range(2 * n):
                moves.append(pltpu.make_async_copy(ref.at[k], sums_out.at[owner(q, steps[place // 2], place % 2)], sems.at[place]))
                place += 1
    j = pl.program_id(0)

    @pl.when(j == 0)
    def _():
        for copy in moves[: -2 * pairs]:
            copy.start()
        first = (me_ref[1] * EXP).astype(F32)
        before = (lax.broadcasted_iota(jnp.int32, (TOK, TOK), 0) < lax.broadcasted_iota(jnp.int32, (TOK, TOK), 1)).astype(BF)
        row = lax.broadcasted_iota(jnp.int32, (PAIR, 2 * TOK), 0).astype(F32)
        for n in range(pairs):
            if split:
                fronts, tails, at = pays[:2], pays[2:], 0
            else:
                fronts = tails = pays[2 * n : 2 * n + 2]
                at = PARTS
            x = jnp.concatenate([jnp.concatenate([ref[i] for i in range(PARTS)], axis=1) for ref in fronts], axis=0)
            g = jnp.concatenate([jnp.concatenate([ref[at + i] for i in range(PARTS)], axis=1) for ref in tails], axis=0)
            named, gate = [], []
            for ref in tails:
                meta_a = ref[at + PARTS, 0:16].astype(F32)
                meta_b = ref[at + PARTS, 16:32].astype(F32)
                ids = meta_a[0:TOP]
                gates = (meta_a[TOP:] + meta_b[0:TOP]) + meta_b[TOP:]
                for e in range(EXP):
                    hit = ids == first + float(e)
                    named.append(jnp.sum(jnp.where(hit, 1.0, 0.0), axis=0, keepdims=True))
                    gate.append(jnp.sum(jnp.where(hit, gates, 0.0), axis=0, keepdims=True))
            mask = jnp.concatenate(named, axis=0)
            rank = dot(mask.astype(BF), before, NN)
            target = jnp.where(mask > 0.5, rank, -1000.0)
            picks, weights = [], []
            for e in range(EXP):
                place = jnp.concatenate([target[e : e + 1], target[EXP + e : EXP + e + 1] + float(CAP)], axis=1)
                gates = jnp.concatenate([gate[e], gate[EXP + e]], axis=1)
                hit = row == place
                picks.append(jnp.where(hit, 1.0, 0.0))
                weights.append(jnp.sum(jnp.where(hit, gates, 0.0), axis=1, keepdims=True))
            pick = jnp.concatenate(picks, axis=0).astype(BF)
            weight = jnp.concatenate(weights, axis=0)
            oh[n] = pick
            x_rows = dot(pick, x, NN).astype(BF)
            s_rows = (dot(pick, g, NN) * weight).astype(BF)
            for e in range(EXP):
                xs[e, n * PAIR : (n + 1) * PAIR] = x_rows[e * PAIR : (e + 1) * PAIR]
                ss[e, n * PAIR : (n + 1) * PAIR] = s_rows[e * PAIR : (e + 1) * PAIR]

    x, s = xs[j], ss[j]
    x_out[0] = x
    s_out[0] = s
    both = dot(x, wgu_ref[0], NN)
    gate_pre, up_val = both[:, :FF], both[:, FF:]
    sig = jax.nn.sigmoid(gate_pre)
    act = gate_pre * sig
    h_out[0] = (act * up_val).astype(BF)
    dh = dot(s, wdn_ref[0], NT)
    d_gate = dh * up_val * sig * (1.0 + gate_pre * (1.0 - sig))
    d_both = jnp.concatenate([d_gate, dh * act], axis=1).astype(BF)
    d_out[0] = d_both
    rg[j] = dot(d_both, wgu_ref[0], NT).astype(BF)

    @pl.when(j == EXP - 1)
    def _():
        for n in range(pairs):
            rows = jnp.concatenate([rg[e, n * PAIR : (n + 1) * PAIR, :] for e in range(EXP)], axis=0)
            sums = dot(oh[n], rows, TN).astype(BF)
            target = stage if last else sums_out
            target[2 * n] = sums[:TOK]
            target[2 * n + 1] = sums[TOK:]
        for copy in moves[-2 * pairs :]:
            copy.start()
        for copy in moves:
            copy.wait()


def work(me, steps, pays, w_gate_up, w_down, earlier=()):
    split = pays[0].shape[0] == PARTS
    pairs = 1 if split else len(pays) // 2
    rows = pairs * PAIR
    widths = (D, D, 2 * FF, FF)
    done = tuple(sums.shape[0] // 2 for sums in earlier)

    def whole(j, me):
        return (0, 0, 0)

    def one(j, me):
        return (j, 0, 0)

    anywhere = pl.BlockSpec(memory_space=pl.ANY)
    once = pl.Buffered(1)
    sums = jax.ShapeDtypeStruct((OWN if done else 2 * pairs, TOK, D), BF)
    return pl.pallas_call(
        functools.partial(work_kernel, pairs, split, done, steps),
        out_shape=tuple(jax.ShapeDtypeStruct((EXP, rows, width), BF) for width in widths) + (sums,),
        grid_spec=pltpu.PrefetchScalarGridSpec(
            num_scalar_prefetch=1,
            grid=(EXP,),
            in_specs=[pl.BlockSpec(pay.shape, whole, pipeline_mode=once) for pay in pays]
            + [pl.BlockSpec((1, D, 2 * FF), one), pl.BlockSpec((1, FF, D), one)]
            + [anywhere] * len(done),
            out_specs=tuple(pl.BlockSpec((1, rows, width), one) for width in widths)
            + (anywhere if done else pl.BlockSpec((2 * pairs, TOK, D), whole),),
            scratch_shapes=[
                pltpu.VMEM((EXP, rows, D), BF),
                pltpu.VMEM((EXP, rows, D), BF),
                pltpu.VMEM((EXP, rows, D), BF),
                pltpu.VMEM((pairs, EXP * PAIR, 2 * TOK), BF),
                pltpu.VMEM((2 * pairs, TOK, D), BF),
                pltpu.SemaphoreType.DMA((OWN,)),
            ],
        ),
        compiler_params=ask(20),
        name="work",
        cost_estimate=pl.CostEstimate(flops=2 * EXP * 256 * D * FF * 8, bytes_accessed=14 * MB, transcendentals=0),
    )(me, *pays, w_gate_up, w_down, *earlier)


def grads_kernel(parts, half, me_ref, *refs):
    chunks, (_, o0, o1, o3, o2a, o2b, _, xa, sa, da, ha, pgu, pdn) = refs[: 4 * len(parts)], refs[4 * len(parts) :]
    jj = pl.program_id(0)
    px, py = me_ref[0] >> 2, me_ref[0] & 3
    low = 0
    for c, rows in enumerate(parts):
        for ref, to in zip(chunks[4 * c : 4 * c + 4], (xa, sa, da, ha)):
            to[low : low + rows] = ref[0]
        low += rows
    pgu[...] = dot(xa[...], da[...], TN)
    pdn[jj] = dot(ha[...], sa[...], TN)

    def outs():
        for first in range(SIDE):
            for second in range(SIDE):
                if first == 2:
                    ref, at = (o2a, second) if second < 2 else (o2b, second - 2)
                else:
                    ref, at = {0: o0, 1: o1, 3: o3}[first], second
                dx, dy = (first, second) if half == 0 else (second, first)
                yield ((px + dx) & 3) * SIDE + ((py + dy) & 3), ref, at

    for step in range(2):

        @pl.when(jj == step)
        def _():
            for number, ref, at in outs():
                base = pl.multiple_of(number * GU_ROWS, GU_ROWS)
                for a in range(4):
                    for b in range(3):
                        n = a * 3 + b
                        top, left = 48 * step + 16 * (n // 4), 256 * (n % 4)
                        ref[at, top : top + 16, left : left + 256] = pgu[pl.ds(base + 16 * a, 16), 256 * b : 256 * b + 256].astype(BF)
                if step == 1:
                    low = pl.multiple_of(number * DN_ROWS, DN_ROWS)
                    ref[at, 96:BLK, :] = jnp.concatenate([pdn[0, pl.ds(low, DN_ROWS), :], pdn[1, pl.ds(low, DN_ROWS), :]], axis=0).astype(BF)


def grads(half, me, chunks, sums):
    parts = tuple(chunk[0].shape[1] for chunk in chunks)
    widths = (D, D, 2 * FF, FF)

    def at(j, w):
        return (2 * half + j, 0, 0)

    def whole(j, w):
        return (0, 0, 0)

    counts = (4, 4, 4, 2, 2)
    return pl.pallas_call(
        functools.partial(grads_kernel, parts, half),
        out_shape=tuple(jax.ShapeDtypeStruct((n, BLK, D), BF) for n in counts) + (jax.ShapeDtypeStruct(sums.shape, BF),),
        grid_spec=pltpu.PrefetchScalarGridSpec(
            num_scalar_prefetch=1,
            grid=(2,),
            in_specs=[pl.BlockSpec((1, rows, width), at) for rows in parts for width in widths] + [pl.BlockSpec(memory_space=pl.ANY)],
            out_specs=tuple(pl.BlockSpec((n, BLK, D), whole) for n in counts) + (pl.BlockSpec(memory_space=pl.ANY),),
            scratch_shapes=[pltpu.VMEM((ROWS, width), BF) for width in widths] + [pltpu.VMEM((D, 2 * FF), F32), pltpu.VMEM((2, FF, D), F32)],
        ),
        input_output_aliases={1 + 4 * len(parts): len(counts)},
        compiler_params=ask(26),
        name="grads",
        cost_estimate=pl.CostEstimate(flops=2 * 2 * ROWS * D * FF * 3, bytes_accessed=12 * MB, transcendentals=0),
    )(me, *[a for chunk in chunks for a in chunk], sums)


def add1_kernel(o1, ra, o3, rb, s1, s3):
    s1[0:2] = (o1[0:2].astype(F32) + ra[...].astype(F32)).astype(BF)
    s1[2:4] = o1[2:4]
    s3[0:2] = o3[0:2]
    s3[2:4] = (o3[2:4].astype(F32) + rb[...].astype(F32)).astype(BF)


def add1(o1, ra, o3, rb):
    out = jax.ShapeDtypeStruct((SIDE, BLK, D), BF)
    return pl.pallas_call(
        add1_kernel,
        out_shape=(out, out),
        compiler_params=ask(12),
        name="add1",
        cost_estimate=pl.CostEstimate(flops=0, bytes_accessed=6 * MB, transcendentals=0),
    )(o1, ra, o3, rb)


def add2_kernel(o0, r1, r3, f0, f1, f3, f2a, f2b):
    def total(k):
        return (o0[k].astype(F32) + r1[k].astype(F32)) + r3[k].astype(F32)

    f0[...] = total(0)
    f1[...] = total(1).astype(BF)
    f3[...] = total(3).astype(BF)
    two = total(2).astype(BF)
    f2a[...] = two[:CUT]
    f2b[...] = two[CUT:]


def add2(o0, r1, r3):
    whole = jax.ShapeDtypeStruct((BLK, D), BF)
    return pl.pallas_call(
        add2_kernel,
        out_shape=(
            jax.ShapeDtypeStruct((BLK, D), F32),
            whole,
            whole,
            jax.ShapeDtypeStruct((CUT, D), BF),
            jax.ShapeDtypeStruct((BLK - CUT, D), BF),
        ),
        compiler_params=ask(12),
        name="add2",
        cost_estimate=pl.CostEstimate(flops=0, bytes_accessed=5 * MB, transcendentals=0),
    )(o0, r1, r3)


def add3_kernel(f1, ra, f3, rb, s1, s3):
    s1[:CUT] = (f1[:CUT].astype(F32) + ra[...].astype(F32)).astype(BF)
    s1[CUT:] = f1[CUT:]
    s3[:CUT] = f3[:CUT]
    s3[CUT:] = (f3[CUT:].astype(F32) + rb[...].astype(F32)).astype(BF)


def add3(f1, ra, f3, rb):
    out = jax.ShapeDtypeStruct((BLK, D), BF)
    return pl.pallas_call(
        add3_kernel,
        out_shape=(out, out),
        compiler_params=ask(12),
        name="add3",
        cost_estimate=pl.CostEstimate(flops=0, bytes_accessed=MB, transcendentals=0),
    )(f1, ra, f3, rb)


def last_kernel(a0, a1, a3, b0, b1, b3, gu_ref, dn_ref):
    for half, (f0, r1, r3) in enumerate(((a0, a1, a3), (b0, b1, b3))):
        total = f0[...] + r1[...].astype(F32) + r3[...].astype(F32)
        for e in range(2):
            j = 2 * half + e
            for a in range(4):
                for b in range(3):
                    n = a * 3 + b
                    top, left = 48 * e + 16 * (n // 4), 256 * (n % 4)
                    gu_ref[16 * a : 16 * a + 16, j, 256 * b : 256 * b + 256] = total[top : top + 16, left : left + 256]
            dn_ref[:, j, :] = total[96 + DN_ROWS * e : 96 + DN_ROWS * (e + 1), :]


def last(*pieces):
    return pl.pallas_call(
        last_kernel,
        out_shape=(
            jax.ShapeDtypeStruct((GU_ROWS, EXP, 2 * FF), F32),
            jax.ShapeDtypeStruct((DN_ROWS, EXP, D), F32),
        ),
        compiler_params=ask(12),
        name="last",
        cost_estimate=pl.CostEstimate(flops=0, bytes_accessed=4 * MB, transcendentals=0),
    )(*pieces)


def along(axis, step):
    pairs = []
    for i in range(SIDE * SIDE):
        x, y = divmod(i, SIDE)
        x, y = ((x + step) % SIDE, y) if axis == 0 else (x, (y + step) % SIDE)
        pairs.append((i, x * SIDE + y))
    return pairs


def move(block, axis, step):
    return lax.ppermute(block, "dp", along(axis, step))


def stage_one(axis, o0, o1, o3, o2a, o2b):
    ra, rb = move(o2a, axis, 1), move(o2b, axis, -1)
    s1, s3 = add1(o1, ra, o3, rb)
    r1, r3 = move(s1, axis, 1), move(s3, axis, -1)
    return add2(o0, r1, r3)


def stage_two(axis, f0, f1, f3, f2a, f2b):
    ra, rb = move(f2a, axis, 1), move(f2b, axis, -1)
    s1, s3 = add3(f1, ra, f3, rb)
    return f0, move(s1, axis, 1), move(s3, axis, -1)


def after(*blocks):
    return lax.optimization_barrier(blocks)[:-1]


def hop(block, step):
    return lax.ppermute(block, "expert", [(i, (i + 2 * step) % OWN) for i in range(OWN)])


def swap(block):
    return lax.ppermute(block, "expert", [(i, i ^ 1) for i in range(OWN)])


def per_device(tokens, out_grad, expert_ids, gates, w_gate_up, w_down):
    me = jnp.stack([lax.axis_index("dp"), lax.axis_index("expert")]).astype(jnp.int32)
    own = prep(me, tokens, out_grad, expert_ids.T, gates.T)
    chunks, sums = [], []

    def run(steps, pays, earlier=()):
        *chunk, total = work(me, steps, pays, w_gate_up, w_down, earlier)
        chunks.append(chunk)
        sums.append(total)

    own_sib = swap(own)
    up, down = hop(own, 1), hop(own, -1)
    run((0,), (own, own_sib))
    up, down = after(up, down, sums[-1])
    for k in range(1, 4):
        pays = (up, swap(up), down, swap(down))
        if k < 3:
            up, down = hop(up, 1), hop(down, -1)
        else:
            x4, g4 = hop(up[:PARTS], 1), hop(down[PARTS:], -1)
        run((-k, k), pays)
        if k < 3:
            up, down = after(up, down, sums[-1])
    x4, g4 = after(x4, g4, sums[-1])
    run((0, -1, 1, -2, 2, -3, 3, 4), (x4, swap(x4), g4, swap(g4)), sums)
    sums = sums[-1]
    *blocks_a, sums = grads(0, me, chunks, sums)
    *blocks_b, sums = grads(1, me, chunks, sums)
    in_grad = lax.psum_scatter(sums.reshape(OWN * TOK, D), "expert", scatter_dimension=0, tiled=True)
    a = stage_two(1, *stage_one(0, *blocks_a))
    b = stage_two(0, *stage_one(1, *blocks_b))
    gu, dn = last(*a, *b)
    return in_grad, gu, dn


def solution(mesh):
    spec = P(("dp", "expert"), None)
    return jax.shard_map(
        per_device,
        mesh=mesh,
        in_specs=(spec, spec, spec, spec, P("expert", None, None), P("expert", None, None)),
        out_specs=(spec, P("dp", "expert", None), P("dp", "expert", None)),
        check_vma=False,
    )
```

```python
import functools

import jax
import jax.numpy as jnp
from jax import lax
from jax.experimental import pallas as pl
from jax.experimental.pallas import tpu as pltpu
from jax.sharding import PartitionSpec as P

TOK = 128
TOP = 8
D = 1024
FF = 384
CAP = 24
EXP = 4
OWN = 16
LINE = 8
SIDE = 4
GU_ROWS = D // 16
DN_ROWS = FF // 16
PAIR = 2 * CAP
ROWS = OWN * CAP
BLK = 2 * (3 * GU_ROWS // 4 + DN_ROWS)
CUT = 80
LANES = 128
PARTS = D // LANES
PAY = 2 * PARTS + 1
BF = jnp.bfloat16
F32 = jnp.float32
MB = 1 << 20


def dot(a, b, dims):
    return lax.dot_general(a, b, (dims, ((), ())), preferred_element_type=F32)


NN = ((1,), (0,))
NT = ((1,), (1,))
TN = ((0,), (0,))


def ask(limit):
    return pltpu.CompilerParams(vmem_limit_bytes=limit * MB)


def prep_kernel(me_ref, x_ref, g_ref, ids_ref, gates_ref, out_ref):
    for i in range(PARTS):
        out_ref[i] = x_ref[:, i * LANES : (i + 1) * LANES]
        out_ref[PARTS + i] = g_ref[:, i * LANES : (i + 1) * LANES]
    gate = gates_ref[...]
    high = gate.astype(BF)
    rest = gate - high.astype(F32)
    mid = rest.astype(BF)
    low = (rest - mid.astype(F32)).astype(BF)
    out_ref[2 * PARTS] = jnp.zeros((TOK, LANES), BF)
    out_ref[2 * PARTS, 0:16] = jnp.concatenate([ids_ref[...].astype(F32).astype(BF), high], axis=0)
    out_ref[2 * PARTS, 16:32] = jnp.concatenate([mid, low], axis=0)


def prep(me, tokens, out_grad, ids_t, gates_t):
    return pl.pallas_call(
        prep_kernel,
        out_shape=jax.ShapeDtypeStruct((PAY, TOK, LANES), BF),
        in_specs=[pl.BlockSpec(memory_space=pltpu.SMEM)] + [pl.BlockSpec(memory_space=pltpu.VMEM)] * 4,
        compiler_params=ask(58),
        name="prep",
        cost_estimate=pl.CostEstimate(flops=0, bytes_accessed=MB, transcendentals=0),
    )(me, tokens, out_grad, ids_t, gates_t)


def pair_kernel(me_ref, own_ref, other_ref, out_ref):
    core = me_ref[1] & 1
    out_ref[core] = own_ref[...]
    out_ref[1 - core] = other_ref[...]


def pair(me, own, other):
    return pl.pallas_call(
        pair_kernel,
        out_shape=jax.ShapeDtypeStruct((2, PAY, TOK, LANES), BF),
        in_specs=[pl.BlockSpec(memory_space=pltpu.SMEM)] + [pl.BlockSpec(memory_space=pltpu.VMEM)] * 2,
        compiler_params=ask(8),
        name="pair",
        cost_estimate=pl.CostEstimate(flops=0, bytes_accessed=2 * MB, transcendentals=0),
    )(me, own, other)


def part_kernel(me_ref, in_ref, out_ref):
    out_ref[...] = in_ref[:, pl.ds((me_ref[1] & 1) * PARTS, PARTS + 1)]


def part(me, block):
    return pl.pallas_call(
        part_kernel,
        out_shape=jax.ShapeDtypeStruct((2, PARTS + 1, TOK, LANES), BF),
        in_specs=[pl.BlockSpec(memory_space=pltpu.SMEM), pl.BlockSpec(memory_space=pltpu.VMEM)],
        compiler_params=ask(8),
        name="part",
        cost_estimate=pl.CostEstimate(flops=0, bytes_accessed=2 * MB, transcendentals=0),
    )(me, block)


def work_kernel(pairs, split, me_ref, *refs):
    count = 2 if split else pairs
    pays, refs = refs[:count], refs[count:]
    wgu_ref, wdn_ref, x_out, s_out, d_out, h_out = refs[:6]
    sums_out = refs[6:-4]
    xs, ss, rg, oh = refs[-4:]
    front = (me_ref[1] & 1) == 0
    j = pl.program_id(0)

    @pl.when(j == 0)
    def _():
        first = (me_ref[1] * EXP).astype(F32)
        before = (lax.broadcasted_iota(jnp.int32, (TOK, TOK), 0) < lax.broadcasted_iota(jnp.int32, (TOK, TOK), 1)).astype(BF)
        row = lax.broadcasted_iota(jnp.int32, (PAIR, 2 * TOK), 0).astype(F32)
        for n in range(pairs):
            if split:

                def take(core, i):
                    if i < PARTS:
                        return jnp.where(front, pays[0][core, i], pays[1][core, i])
                    return jnp.where(front, pays[1][core, i - PARTS], pays[0][core, i - PARTS])

            else:

                def take(core, i, ref=pays[n]):
                    return ref[core, i]

            x = jnp.concatenate([jnp.concatenate([take(core, i) for i in range(PARTS)], axis=1) for core in range(2)], axis=0)
            g = jnp.concatenate([jnp.concatenate([take(core, PARTS + i) for i in range(PARTS)], axis=1) for core in range(2)], axis=0)
            named, gate = [], []
            for core in range(2):
                meta = take(core, 2 * PARTS)[0:32].astype(F32)
                meta_a, meta_b = meta[0:16], meta[16:32]
                ids = meta_a[0:TOP]
                gates = (meta_a[TOP:] + meta_b[0:TOP]) + meta_b[TOP:]
                for e in range(EXP):
                    hit = ids == first + float(e)
                    named.append(jnp.sum(jnp.where(hit, 1.0, 0.0), axis=0, keepdims=True))
                    gate.append(jnp.sum(jnp.where(hit, gates, 0.0), axis=0, keepdims=True))
            mask = jnp.concatenate(named, axis=0)
            rank = dot(mask.astype(BF), before, NN)
            target = jnp.where(mask > 0.5, rank, -1000.0)
            picks, weights = [], []
            for e in range(EXP):
                place = jnp.concatenate([target[e : e + 1], target[EXP + e : EXP + e + 1] + float(CAP)], axis=1)
                gates = jnp.concatenate([gate[e], gate[EXP + e]], axis=1)
                hit = row == place
                picks.append(jnp.where(hit, 1.0, 0.0))
                weights.append(jnp.sum(jnp.where(hit, gates, 0.0), axis=1, keepdims=True))
            pick = jnp.concatenate(picks, axis=0).astype(BF)
            weight = jnp.concatenate(weights, axis=0)
            oh[n] = pick
            x_rows = dot(pick, x, NN).astype(BF)
            s_rows = (dot(pick, g, NN) * weight).astype(BF)
            for e in range(EXP):
                xs[e, n * PAIR : (n + 1) * PAIR] = x_rows[e * PAIR : (e + 1) * PAIR]
                ss[e, n * PAIR : (n + 1) * PAIR] = s_rows[e * PAIR : (e + 1) * PAIR]

    x, s = xs[j], ss[j]
    x_out[0] = x
    s_out[0] = s
    both = dot(x, wgu_ref[0], NN)
    gate_pre, up_val = both[:, :FF], both[:, FF:]
    sig = jax.nn.sigmoid(gate_pre)
    act = gate_pre * sig
    h_out[0] = (act * up_val).astype(BF)
    dh = dot(s, wdn_ref[0], NT)
    d_gate = dh * up_val * sig * (1.0 + gate_pre * (1.0 - sig))
    d_both = jnp.concatenate([d_gate, dh * act], axis=1).astype(BF)
    d_out[0] = d_both
    rg[j] = dot(d_both, wgu_ref[0], NT).astype(BF)

    @pl.when(j == EXP - 1)
    def _():
        for n in range(pairs):
            rows = jnp.concatenate([rg[e, n * PAIR : (n + 1) * PAIR, :] for e in range(EXP)], axis=0)
            sums = dot(oh[n], rows, TN).astype(BF)
            if split:
                sums_out[0][...] = jnp.where(front, sums[TOK:], sums[:TOK])
                sums_out[1][...] = jnp.where(front, sums[:TOK], sums[TOK:])
            else:
                sums_out[n][0] = sums[:TOK]
                sums_out[n][1] = sums[TOK:]


def work(me, pays, w_gate_up, w_down):
    split = pays[0].shape[1] != PAY
    pairs = 1 if split else len(pays)
    rows = pairs * PAIR
    widths = (D, D, 2 * FF, FF)

    def one(j, me):
        return (j, 0, 0)

    shape = (TOK, D) if split else (2, TOK, D)
    once = pl.Buffered(1)
    return pl.pallas_call(
        functools.partial(work_kernel, pairs, split),
        out_shape=tuple(jax.ShapeDtypeStruct((EXP, rows, width), BF) for width in widths)
        + (jax.ShapeDtypeStruct(shape, BF),) * len(pays),
        grid_spec=pltpu.PrefetchScalarGridSpec(
            num_scalar_prefetch=1,
            grid=(EXP,),
            in_specs=[pl.BlockSpec(pay.shape, lambda j, me: (0, 0, 0, 0), pipeline_mode=once) for pay in pays]
            + [pl.BlockSpec((1, D, 2 * FF), one), pl.BlockSpec((1, FF, D), one)],
            out_specs=tuple(pl.BlockSpec((1, rows, width), one) for width in widths)
            + (pl.BlockSpec(shape, lambda j, me: (0,) * len(shape)),) * len(pays),
            scratch_shapes=[
                pltpu.VMEM((EXP, rows, D), BF),
                pltpu.VMEM((EXP, rows, D), BF),
                pltpu.VMEM((EXP, rows, D), BF),
                pltpu.VMEM((pairs, EXP * PAIR, 2 * TOK), BF),
            ],
        ),
        compiler_params=ask(20),
        name="work",
        cost_estimate=pl.CostEstimate(flops=2 * EXP * 256 * D * FF * 8, bytes_accessed=14 * MB, transcendentals=0),
    )(me, *pays, w_gate_up, w_down)


def grads_kernel(parts, half, me_ref, *refs):
    chunks, (o0, o1, o3, o2a, o2b, xa, sa, da, ha, pgu, pdn) = refs[: 4 * len(parts)], refs[4 * len(parts) :]
    jj = pl.program_id(0)
    px, py = me_ref[0] >> 2, me_ref[0] & 3
    low = 0
    for c, rows in enumerate(parts):
        for ref, to in zip(chunks[4 * c : 4 * c + 4], (xa, sa, da, ha)):
            to[low : low + rows] = ref[0]
        low += rows
    pgu[...] = dot(xa[...], da[...], TN)
    pdn[jj] = dot(ha[...], sa[...], TN)

    def outs():
        for first in range(SIDE):
            for second in range(SIDE):
                if first == 2:
                    ref, at = (o2a, second) if second < 2 else (o2b, second - 2)
                else:
                    ref, at = {0: o0, 1: o1, 3: o3}[first], second
                dx, dy = (first, second) if half == 0 else (second, first)
                yield ((px + dx) & 3) * SIDE + ((py + dy) & 3), ref, at

    for step in range(2):

        @pl.when(jj == step)
        def _():
            for number, ref, at in outs():
                base = pl.multiple_of(number * GU_ROWS, GU_ROWS)
                for a in range(4):
                    for b in range(3):
                        n = a * 3 + b
                        top, left = 48 * step + 16 * (n // 4), 256 * (n % 4)
                        ref[at, top : top + 16, left : left + 256] = pgu[pl.ds(base + 16 * a, 16), 256 * b : 256 * b + 256].astype(BF)
                if step == 1:
                    low = pl.multiple_of(number * DN_ROWS, DN_ROWS)
                    ref[at, 96:BLK, :] = jnp.concatenate([pdn[0, pl.ds(low, DN_ROWS), :], pdn[1, pl.ds(low, DN_ROWS), :]], axis=0).astype(BF)


def grads(half, me, chunks):
    parts = tuple(chunk[0].shape[1] for chunk in chunks)
    widths = (D, D, 2 * FF, FF)

    def at(j, w):
        return (2 * half + j, 0, 0)

    def whole(j, w):
        return (0, 0, 0)

    counts = (4, 4, 4, 2, 2)
    return pl.pallas_call(
        functools.partial(grads_kernel, parts, half),
        out_shape=tuple(jax.ShapeDtypeStruct((n, BLK, D), BF) for n in counts),
        grid_spec=pltpu.PrefetchScalarGridSpec(
            num_scalar_prefetch=1,
            grid=(2,),
            in_specs=[pl.BlockSpec((1, rows, width), at) for rows in parts for width in widths],
            out_specs=tuple(pl.BlockSpec((n, BLK, D), whole) for n in counts),
            scratch_shapes=[pltpu.VMEM((ROWS, width), BF) for width in widths] + [pltpu.VMEM((D, 2 * FF), F32), pltpu.VMEM((2, FF, D), F32)],
        ),
        compiler_params=ask(26),
        name="grads",
        cost_estimate=pl.CostEstimate(flops=2 * 2 * ROWS * D * FF * 3, bytes_accessed=12 * MB, transcendentals=0),
    )(me, *[a for chunk in chunks for a in chunk])


def far_kernel(mine_ref, got_ref, out_ref):
    out_ref[...] = (mine_ref[...].astype(F32) + got_ref[...].astype(F32)).astype(BF)


def far(mine, got):
    return pl.pallas_call(
        far_kernel,
        out_shape=jax.ShapeDtypeStruct((TOK, D), BF),
        compiler_params=ask(8),
        name="far",
        cost_estimate=pl.CostEstimate(flops=0, bytes_accessed=MB, transcendentals=0),
    )(mine, got)


def near_kernel(me_ref, mine_ref, got_ref, came_ref, out_ref):
    if len(came_ref.shape) == 3:
        out_ref[...] = ((mine_ref[...].astype(F32) + got_ref[...].astype(F32)) + came_ref[...].astype(F32)).astype(BF)
    else:
        core = me_ref[1] & 1
        out_ref[core] = ((mine_ref[core].astype(F32) + got_ref[core].astype(F32)) + came_ref[...].astype(F32)).astype(BF)
        out_ref[1 - core] = (mine_ref[1 - core].astype(F32) + got_ref[1 - core].astype(F32)).astype(BF)


def near(me, mine, got, came):
    return pl.pallas_call(
        near_kernel,
        out_shape=jax.ShapeDtypeStruct((2, TOK, D), BF),
        in_specs=[pl.BlockSpec(memory_space=pltpu.SMEM)] + [pl.BlockSpec(memory_space=pltpu.VMEM)] * 3,
        compiler_params=ask(8),
        name="near",
        cost_estimate=pl.CostEstimate(flops=0, bytes_accessed=2 * MB, transcendentals=0),
    )(me, mine, got, came)


def home_kernel(me_ref, mine_ref, came_ref, keep_ref, give_a, give_b):
    core = me_ref[1] & 1
    keep_ref[...] = mine_ref[core].astype(F32) + came_ref[core].astype(F32)
    give = (mine_ref[1 - core].astype(F32) + came_ref[1 - core].astype(F32)).astype(BF)
    give_a[...] = give[: TOK // 2]
    give_b[...] = give[TOK // 2 :]


def home(me, mine, came):
    return pl.pallas_call(
        home_kernel,
        out_shape=(jax.ShapeDtypeStruct((TOK, D), F32),) + (jax.ShapeDtypeStruct((TOK // 2, D), BF),) * 2,
        in_specs=[pl.BlockSpec(memory_space=pltpu.SMEM)] + [pl.BlockSpec(memory_space=pltpu.VMEM)] * 2,
        compiler_params=ask(8),
        name="home",
        cost_estimate=pl.CostEstimate(flops=0, bytes_accessed=MB, transcendentals=0),
    )(me, mine, came)


def done_kernel(mine_ref, a_ref, b_ref, out_ref):
    half = TOK // 2
    out_ref[:half] = (mine_ref[:half] + a_ref[...].astype(F32)).astype(BF)
    out_ref[half:] = (mine_ref[half:] + b_ref[...].astype(F32)).astype(BF)


def done(mine, a, b):
    return pl.pallas_call(
        done_kernel,
        out_shape=jax.ShapeDtypeStruct((TOK, D), BF),
        compiler_params=ask(8),
        name="done",
        cost_estimate=pl.CostEstimate(flops=0, bytes_accessed=MB, transcendentals=0),
    )(mine, a, b)


def add1_kernel(o1, ra, o3, rb, s1, s3):
    s1[0:2] = (o1[0:2].astype(F32) + ra[...].astype(F32)).astype(BF)
    s1[2:4] = o1[2:4]
    s3[0:2] = o3[0:2]
    s3[2:4] = (o3[2:4].astype(F32) + rb[...].astype(F32)).astype(BF)


def add1(o1, ra, o3, rb):
    out = jax.ShapeDtypeStruct((SIDE, BLK, D), BF)
    return pl.pallas_call(
        add1_kernel,
        out_shape=(out, out),
        compiler_params=ask(12),
        name="add1",
        cost_estimate=pl.CostEstimate(flops=0, bytes_accessed=6 * MB, transcendentals=0),
    )(o1, ra, o3, rb)


def add2_kernel(o0, r1, r3, f0, f1, f3, f2a, f2b):
    def total(k):
        return (o0[k].astype(F32) + r1[k].astype(F32)) + r3[k].astype(F32)

    f0[...] = total(0)
    f1[...] = total(1).astype(BF)
    f3[...] = total(3).astype(BF)
    two = total(2).astype(BF)
    f2a[...] = two[:CUT]
    f2b[...] = two[CUT:]


def add2(o0, r1, r3):
    whole = jax.ShapeDtypeStruct((BLK, D), BF)
    return pl.pallas_call(
        add2_kernel,
        out_shape=(
            jax.ShapeDtypeStruct((BLK, D), F32),
            whole,
            whole,
            jax.ShapeDtypeStruct((CUT, D), BF),
            jax.ShapeDtypeStruct((BLK - CUT, D), BF),
        ),
        compiler_params=ask(12),
        name="add2",
        cost_estimate=pl.CostEstimate(flops=0, bytes_accessed=5 * MB, transcendentals=0),
    )(o0, r1, r3)


def add3_kernel(f1, ra, f3, rb, s1, s3):
    s1[:CUT] = (f1[:CUT].astype(F32) + ra[...].astype(F32)).astype(BF)
    s1[CUT:] = f1[CUT:]
    s3[:CUT] = f3[:CUT]
    s3[CUT:] = (f3[CUT:].astype(F32) + rb[...].astype(F32)).astype(BF)


def add3(f1, ra, f3, rb):
    out = jax.ShapeDtypeStruct((BLK, D), BF)
    return pl.pallas_call(
        add3_kernel,
        out_shape=(out, out),
        compiler_params=ask(12),
        name="add3",
        cost_estimate=pl.CostEstimate(flops=0, bytes_accessed=MB, transcendentals=0),
    )(f1, ra, f3, rb)


def last_kernel(a0, a1, a3, b0, b1, b3, gu_ref, dn_ref):
    for half, (f0, r1, r3) in enumerate(((a0, a1, a3), (b0, b1, b3))):
        total = f0[...] + r1[...].astype(F32) + r3[...].astype(F32)
        for e in range(2):
            j = 2 * half + e
            for a in range(4):
                for b in range(3):
                    n = a * 3 + b
                    top, left = 48 * e + 16 * (n // 4), 256 * (n % 4)
                    gu_ref[16 * a : 16 * a + 16, j, 256 * b : 256 * b + 256] = total[top : top + 16, left : left + 256]
            dn_ref[:, j, :] = total[96 + DN_ROWS * e : 96 + DN_ROWS * (e + 1), :]


def last(*pieces):
    return pl.pallas_call(
        last_kernel,
        out_shape=(
            jax.ShapeDtypeStruct((GU_ROWS, EXP, 2 * FF), F32),
            jax.ShapeDtypeStruct((DN_ROWS, EXP, D), F32),
        ),
        compiler_params=ask(12),
        name="last",
        cost_estimate=pl.CostEstimate(flops=0, bytes_accessed=4 * MB, transcendentals=0),
    )(*pieces)


def along(axis, step):
    pairs = []
    for i in range(SIDE * SIDE):
        x, y = divmod(i, SIDE)
        x, y = ((x + step) % SIDE, y) if axis == 0 else (x, (y + step) % SIDE)
        pairs.append((i, x * SIDE + y))
    return pairs


def move(block, axis, step):
    return lax.ppermute(block, "dp", along(axis, step))


def stage_one(axis, o0, o1, o3, o2a, o2b):
    ra, rb = move(o2a, axis, 1), move(o2b, axis, -1)
    s1, s3 = add1(o1, ra, o3, rb)
    r1, r3 = move(s1, axis, 1), move(s3, axis, -1)
    return list(add2(o0, r1, r3))


def stage_two(axis, f0, f1, f3, f2a, f2b):
    ra, rb = move(f2a, axis, 1), move(f2b, axis, -1)
    s1, s3 = add3(f1, ra, f3, rb)
    return f0, move(s1, axis, 1), move(s3, axis, -1)


def after(*blocks):
    return lax.optimization_barrier(blocks)[0]


def hop(block):
    pairs = []
    for i in range(OWN):
        z, core = divmod(i, 2)
        pairs.append((i, 2 * ((z + 1 - 2 * core) % LINE) + core))
    return lax.ppermute(block, "expert", pairs)


def swap(block):
    return lax.ppermute(block, "expert", [(i, i ^ 1) for i in range(OWN)])


def per_device(tokens, out_grad, expert_ids, gates, w_gate_up, w_down):
    me = jnp.stack([lax.axis_index("dp"), lax.axis_index("expert")]).astype(jnp.int32)
    own = prep(me, tokens, out_grad, expert_ids.T, gates.T)
    chunks, mine, got = [], [], []

    def run(pays):
        *chunk, keep = work(me, pays, w_gate_up, w_down)
        chunks.append(chunk[:4])
        mine.append(keep)
        got.extend(swap(give) for give in chunk[4:])

    near_by = pair(me, own, swap(own))
    came = hop(near_by)
    run((near_by,))
    came = after(came, mine[-1])
    for k in range(1, 4):
        pays = (came, swap(came))
        came = hop(came if k < 3 else part(me, came))
        run(pays)
        came = after(came, got[-1] if k < 3 else mine[-1])
    run((came, swap(came)))
    blocks_a = grads(0, me, chunks)
    blocks_b = grads(1, me, chunks)
    came = hop(far(mine[4], got[3]))
    for k in (3, 2, 1):
        came = hop(near(me, mine[k], got[k - 1], came))
    keep, *give = home(me, mine[0], came)
    in_grad = done(keep, *[swap(half) for half in give])
    a, b = stage_one(0, *blocks_a), stage_one(1, *blocks_b)
    a[3], a[4] = after(a[3], b[3]), after(a[4], b[3])
    b[3], b[4] = after(b[3], a[3]), after(b[4], a[4])
    a, b = stage_two(1, *a), stage_two(0, *b)
    gu, dn = last(*a, *b)
    return in_grad, gu, dn


def solution(mesh):
    spec = P(("dp", "expert"), None)
    return jax.shard_map(
        per_device,
        mesh=mesh,
        in_specs=(spec, spec, spec, spec, P("expert", None, None), P("expert", None, None)),
        out_specs=(spec, P("dp", "expert", None), P("dp", "expert", None)),
        check_vma=False,
    )
```

```python
import functools

import jax
import jax.numpy as jnp
from jax import lax
from jax.experimental import pallas as pl
from jax.experimental.pallas import tpu as pltpu
from jax.sharding import PartitionSpec as P

TOK = 128
TOP = 8
D = 1024
FF = 384
CAP = 24
EXP = 4
OWN = 16
LINE = 8
SIDE = 4
GU_ROWS = D // 16
DN_ROWS = FF // 16
PAIR = 2 * CAP
ROWS = OWN * CAP
BLK = 2 * (3 * GU_ROWS // 4 + DN_ROWS)
CUT = 80
LANES = 128
PARTS = D // LANES
PAY = 2 * PARTS + 1
BF = jnp.bfloat16
F32 = jnp.float32
MB = 1 << 20


def dot(a, b, dims):
    return lax.dot_general(a, b, (dims, ((), ())), preferred_element_type=F32)


NN = ((1,), (0,))
NT = ((1,), (1,))
TN = ((0,), (0,))


def ask(limit):
    return pltpu.CompilerParams(vmem_limit_bytes=limit * MB)


def prep_kernel(me_ref, x_ref, g_ref, ids_ref, gates_ref, out_ref):
    for i in range(PARTS):
        out_ref[i] = x_ref[:, i * LANES : (i + 1) * LANES]
        out_ref[PARTS + i] = g_ref[:, i * LANES : (i + 1) * LANES]
    gate = gates_ref[...]
    high = gate.astype(BF)
    rest = gate - high.astype(F32)
    mid = rest.astype(BF)
    low = (rest - mid.astype(F32)).astype(BF)
    out_ref[2 * PARTS] = jnp.zeros((TOK, LANES), BF)
    out_ref[2 * PARTS, 0:16] = jnp.concatenate([ids_ref[...].astype(F32).astype(BF), high], axis=0)
    out_ref[2 * PARTS, 16:32] = jnp.concatenate([mid, low], axis=0)


def prep(me, tokens, out_grad, ids_t, gates_t):
    return pl.pallas_call(
        prep_kernel,
        out_shape=jax.ShapeDtypeStruct((PAY, TOK, LANES), BF),
        in_specs=[pl.BlockSpec(memory_space=pltpu.SMEM)] + [pl.BlockSpec(memory_space=pltpu.VMEM)] * 4,
        compiler_params=ask(58),
        name="prep",
        cost_estimate=pl.CostEstimate(flops=0, bytes_accessed=MB, transcendentals=0),
    )(me, tokens, out_grad, ids_t, gates_t)


def pair_kernel(me_ref, own_ref, other_ref, out_ref):
    core = me_ref[1] & 1
    out_ref[core] = own_ref[...]
    out_ref[1 - core] = other_ref[...]


def pair(me, own, other):
    return pl.pallas_call(
        pair_kernel,
        out_shape=jax.ShapeDtypeStruct((2, PAY, TOK, LANES), BF),
        in_specs=[pl.BlockSpec(memory_space=pltpu.SMEM)] + [pl.BlockSpec(memory_space=pltpu.VMEM)] * 2,
        compiler_params=ask(8),
        name="pair",
        cost_estimate=pl.CostEstimate(flops=0, bytes_accessed=2 * MB, transcendentals=0),
    )(me, own, other)


def part_kernel(me_ref, in_ref, out_ref):
    out_ref[...] = in_ref[:, pl.ds((me_ref[1] & 1) * PARTS, PARTS + 1)]


def part(me, block):
    return pl.pallas_call(
        part_kernel,
        out_shape=jax.ShapeDtypeStruct((2, PARTS + 1, TOK, LANES), BF),
        in_specs=[pl.BlockSpec(memory_space=pltpu.SMEM), pl.BlockSpec(memory_space=pltpu.VMEM)],
        compiler_params=ask(8),
        name="part",
        cost_estimate=pl.CostEstimate(flops=0, bytes_accessed=2 * MB, transcendentals=0),
    )(me, block)


def work_kernel(pairs, split, me_ref, *refs):
    count = 2 if split else pairs
    pays, refs = refs[:count], refs[count:]
    wgu_ref, wdn_ref, x_out, s_out, d_out, h_out = refs[:6]
    sums_out = refs[6:-4]
    xs, ss, rg, oh = refs[-4:]
    front = (me_ref[1] & 1) == 0
    j = pl.program_id(0)

    @pl.when(j == 0)
    def _():
        first = (me_ref[1] * EXP).astype(F32)
        before = (lax.broadcasted_iota(jnp.int32, (TOK, TOK), 0) < lax.broadcasted_iota(jnp.int32, (TOK, TOK), 1)).astype(BF)
        row = lax.broadcasted_iota(jnp.int32, (PAIR, 2 * TOK), 0).astype(F32)
        for n in range(pairs):
            if split:

                def take(core, i):
                    if i < PARTS:
                        return jnp.where(front, pays[0][core, i], pays[1][core, i])
                    return jnp.where(front, pays[1][core, i - PARTS], pays[0][core, i - PARTS])

            else:

                def take(core, i, ref=pays[n]):
                    return ref[core, i]

            x = jnp.concatenate([jnp.concatenate([take(core, i) for i in range(PARTS)], axis=1) for core in range(2)], axis=0)
            g = jnp.concatenate([jnp.concatenate([take(core, PARTS + i) for i in range(PARTS)], axis=1) for core in range(2)], axis=0)
            named, gate = [], []
            for core in range(2):
                meta = take(core, 2 * PARTS)[0:32].astype(F32)
                meta_a, meta_b = meta[0:16], meta[16:32]
                ids = meta_a[0:TOP]
                gates = (meta_a[TOP:] + meta_b[0:TOP]) + meta_b[TOP:]
                for e in range(EXP):
                    hit = ids == first + float(e)
                    named.append(jnp.sum(jnp.where(hit, 1.0, 0.0), axis=0, keepdims=True))
                    gate.append(jnp.sum(jnp.where(hit, gates, 0.0), axis=0, keepdims=True))
            mask = jnp.concatenate(named, axis=0)
            rank = dot(mask.astype(BF), before, NN)
            target = jnp.where(mask > 0.5, rank, -1000.0)
            picks, weights = [], []
            for e in range(EXP):
                place = jnp.concatenate([target[e : e + 1], target[EXP + e : EXP + e + 1] + float(CAP)], axis=1)
                gates = jnp.concatenate([gate[e], gate[EXP + e]], axis=1)
                hit = row == place
                picks.append(jnp.where(hit, 1.0, 0.0))
                weights.append(jnp.sum(jnp.where(hit, gates, 0.0), axis=1, keepdims=True))
            pick = jnp.concatenate(picks, axis=0).astype(BF)
            weight = jnp.concatenate(weights, axis=0)
            oh[n] = pick
            x_rows = dot(pick, x, NN).astype(BF)
            s_rows = (dot(pick, g, NN) * weight).astype(BF)
            for e in range(EXP):
                xs[e, n * PAIR : (n + 1) * PAIR] = x_rows[e * PAIR : (e + 1) * PAIR]
                ss[e, n * PAIR : (n + 1) * PAIR] = s_rows[e * PAIR : (e + 1) * PAIR]

    x, s = xs[j], ss[j]
    x_out[0] = x
    s_out[0] = s
    both = dot(x, wgu_ref[0], NN)
    gate_pre, up_val = both[:, :FF], both[:, FF:]
    sig = jax.nn.sigmoid(gate_pre)
    act = gate_pre * sig
    h_out[0] = (act * up_val).astype(BF)
    dh = dot(s, wdn_ref[0], NT)
    d_gate = dh * up_val * sig * (1.0 + gate_pre * (1.0 - sig))
    d_both = jnp.concatenate([d_gate, dh * act], axis=1).astype(BF)
    d_out[0] = d_both
    rg[j] = dot(d_both, wgu_ref[0], NT).astype(BF)

    @pl.when(j == EXP - 1)
    def _():
        for n in range(pairs):
            rows = jnp.concatenate([rg[e, n * PAIR : (n + 1) * PAIR, :] for e in range(EXP)], axis=0)
            sums = dot(oh[n], rows, TN).astype(BF)
            if split:
                sums_out[0][...] = jnp.where(front, sums[TOK:], sums[:TOK])
                sums_out[1][...] = jnp.where(front, sums[:TOK], sums[TOK:])
            else:
                sums_out[n][0] = sums[:TOK]
                sums_out[n][1] = sums[TOK:]


def work(me, pays, w_gate_up, w_down):
    split = pays[0].shape[1] != PAY
    pairs = 1 if split else len(pays)
    rows = pairs * PAIR
    widths = (D, D, 2 * FF, FF)

    def one(j, me):
        return (j, 0, 0)

    shape = (TOK, D) if split else (2, TOK, D)
    once = pl.Buffered(1)
    return pl.pallas_call(
        functools.partial(work_kernel, pairs, split),
        out_shape=tuple(jax.ShapeDtypeStruct((EXP, rows, width), BF) for width in widths)
        + (jax.ShapeDtypeStruct(shape, BF),) * len(pays),
        grid_spec=pltpu.PrefetchScalarGridSpec(
            num_scalar_prefetch=1,
            grid=(EXP,),
            in_specs=[pl.BlockSpec(pay.shape, lambda j, me: (0, 0, 0, 0), pipeline_mode=once) for pay in pays]
            + [pl.BlockSpec((1, D, 2 * FF), one), pl.BlockSpec((1, FF, D), one)],
            out_specs=tuple(pl.BlockSpec((1, rows, width), one) for width in widths)
            + (pl.BlockSpec(shape, lambda j, me: (0,) * len(shape)),) * len(pays),
            scratch_shapes=[
                pltpu.VMEM((EXP, rows, D), BF),
                pltpu.VMEM((EXP, rows, D), BF),
                pltpu.VMEM((EXP, rows, D), BF),
                pltpu.VMEM((pairs, EXP * PAIR, 2 * TOK), BF),
            ],
        ),
        compiler_params=ask(20),
        name="work",
        cost_estimate=pl.CostEstimate(flops=2 * EXP * 256 * D * FF * 8, bytes_accessed=14 * MB, transcendentals=0),
    )(me, *pays, w_gate_up, w_down)


def grads_kernel(parts, half, me_ref, *refs):
    chunks, (o0, o1, o3, o2a, o2b, xa, sa, da, ha, pgu, pdn) = refs[: 4 * len(parts)], refs[4 * len(parts) :]
    jj = pl.program_id(0)
    px, py = me_ref[0] >> 2, me_ref[0] & 3
    low = 0
    for c, rows in enumerate(parts):
        for ref, to in zip(chunks[4 * c : 4 * c + 4], (xa, sa, da, ha)):
            to[low : low + rows] = ref[0]
        low += rows
    pgu[...] = dot(xa[...], da[...], TN)
    pdn[jj] = dot(ha[...], sa[...], TN)

    def outs():
        for first in range(SIDE):
            for second in range(SIDE):
                if first == 2:
                    ref, at = (o2a, second) if second < 2 else (o2b, second - 2)
                else:
                    ref, at = {0: o0, 1: o1, 3: o3}[first], second
                dx, dy = (first, second) if half == 0 else (second, first)
                yield ((px + dx) & 3) * SIDE + ((py + dy) & 3), ref, at

    for step in range(2):

        @pl.when(jj == step)
        def _():
            for number, ref, at in outs():
                base = pl.multiple_of(number * GU_ROWS, GU_ROWS)
                for a in range(4):
                    for b in range(3):
                        n = a * 3 + b
                        top, left = 48 * step + 16 * (n // 4), 256 * (n % 4)
                        ref[at, top : top + 16, left : left + 256] = pgu[pl.ds(base + 16 * a, 16), 256 * b : 256 * b + 256].astype(BF)
                if step == 1:
                    low = pl.multiple_of(number * DN_ROWS, DN_ROWS)
                    ref[at, 96:BLK, :] = jnp.concatenate([pdn[0, pl.ds(low, DN_ROWS), :], pdn[1, pl.ds(low, DN_ROWS), :]], axis=0).astype(BF)


def grads(half, me, chunks):
    parts = tuple(chunk[0].shape[1] for chunk in chunks)
    widths = (D, D, 2 * FF, FF)

    def at(j, w):
        return (2 * half + j, 0, 0)

    def whole(j, w):
        return (0, 0, 0)

    counts = (4, 4, 4, 2, 2)
    return pl.pallas_call(
        functools.partial(grads_kernel, parts, half),
        out_shape=tuple(jax.ShapeDtypeStruct((n, BLK, D), BF) for n in counts),
        grid_spec=pltpu.PrefetchScalarGridSpec(
            num_scalar_prefetch=1,
            grid=(2,),
            in_specs=[pl.BlockSpec((1, rows, width), at) for rows in parts for width in widths],
            out_specs=tuple(pl.BlockSpec((n, BLK, D), whole) for n in counts),
            scratch_shapes=[pltpu.VMEM((ROWS, width), BF) for width in widths] + [pltpu.VMEM((D, 2 * FF), F32), pltpu.VMEM((2, FF, D), F32)],
        ),
        compiler_params=ask(26),
        name="grads",
        cost_estimate=pl.CostEstimate(flops=2 * 2 * ROWS * D * FF * 3, bytes_accessed=12 * MB, transcendentals=0),
    )(me, *[a for chunk in chunks for a in chunk])


def far_kernel(mine_ref, got_ref, out_ref):
    out_ref[...] = (mine_ref[...].astype(F32) + got_ref[...].astype(F32)).astype(BF)


def far(mine, got):
    return pl.pallas_call(
        far_kernel,
        out_shape=jax.ShapeDtypeStruct((TOK, D), BF),
        compiler_params=ask(8),
        name="far",
        cost_estimate=pl.CostEstimate(flops=0, bytes_accessed=MB, transcendentals=0),
    )(mine, got)


def near_kernel(me_ref, mine_ref, got_ref, came_ref, out_ref):
    if len(came_ref.shape) == 3:
        out_ref[...] = ((mine_ref[...].astype(F32) + got_ref[...].astype(F32)) + came_ref[...].astype(F32)).astype(BF)
    else:
        core = me_ref[1] & 1
        out_ref[core] = ((mine_ref[core].astype(F32) + got_ref[core].astype(F32)) + came_ref[...].astype(F32)).astype(BF)
        out_ref[1 - core] = (mine_ref[1 - core].astype(F32) + got_ref[1 - core].astype(F32)).astype(BF)


def near(me, mine, got, came):
    return pl.pallas_call(
        near_kernel,
        out_shape=jax.ShapeDtypeStruct((2, TOK, D), BF),
        in_specs=[pl.BlockSpec(memory_space=pltpu.SMEM)] + [pl.BlockSpec(memory_space=pltpu.VMEM)] * 3,
        compiler_params=ask(8),
        name="near",
        cost_estimate=pl.CostEstimate(flops=0, bytes_accessed=2 * MB, transcendentals=0),
    )(me, mine, got, came)


def home_kernel(me_ref, mine_ref, came_ref, keep_ref, give_a, give_b):
    core = me_ref[1] & 1
    keep_ref[...] = mine_ref[core].astype(F32) + came_ref[core].astype(F32)
    give = (mine_ref[1 - core].astype(F32) + came_ref[1 - core].astype(F32)).astype(BF)
    give_a[...] = give[: TOK // 2]
    give_b[...] = give[TOK // 2 :]


def home(me, mine, came):
    return pl.pallas_call(
        home_kernel,
        out_shape=(jax.ShapeDtypeStruct((TOK, D), F32),) + (jax.ShapeDtypeStruct((TOK // 2, D), BF),) * 2,
        in_specs=[pl.BlockSpec(memory_space=pltpu.SMEM)] + [pl.BlockSpec(memory_space=pltpu.VMEM)] * 2,
        compiler_params=ask(8),
        name="home",
        cost_estimate=pl.CostEstimate(flops=0, bytes_accessed=MB, transcendentals=0),
    )(me, mine, came)


def done_kernel(mine_ref, a_ref, b_ref, out_ref):
    half = TOK // 2
    out_ref[:half] = (mine_ref[:half] + a_ref[...].astype(F32)).astype(BF)
    out_ref[half:] = (mine_ref[half:] + b_ref[...].astype(F32)).astype(BF)


def done(mine, a, b):
    return pl.pallas_call(
        done_kernel,
        out_shape=jax.ShapeDtypeStruct((TOK, D), BF),
        compiler_params=ask(8),
        name="done",
        cost_estimate=pl.CostEstimate(flops=0, bytes_accessed=MB, transcendentals=0),
    )(mine, a, b)


def add1_kernel(o1, ra, o3, rb, s1, s3):
    s1[0:2] = (o1[0:2].astype(F32) + ra[...].astype(F32)).astype(BF)
    s1[2:4] = o1[2:4]
    s3[0:2] = o3[0:2]
    s3[2:4] = (o3[2:4].astype(F32) + rb[...].astype(F32)).astype(BF)


def add1(o1, ra, o3, rb):
    out = jax.ShapeDtypeStruct((SIDE, BLK, D), BF)
    return pl.pallas_call(
        add1_kernel,
        out_shape=(out, out),
        compiler_params=ask(12),
        name="add1",
        cost_estimate=pl.CostEstimate(flops=0, bytes_accessed=6 * MB, transcendentals=0),
    )(o1, ra, o3, rb)


def add2_kernel(o0, r1, r3, f0, f1, f3, f2a, f2b):
    def total(k):
        return (o0[k].astype(F32) + r1[k].astype(F32)) + r3[k].astype(F32)

    f0[...] = total(0)
    f1[...] = total(1).astype(BF)
    f3[...] = total(3).astype(BF)
    two = total(2).astype(BF)
    f2a[...] = two[:CUT]
    f2b[...] = two[CUT:]


def add2(o0, r1, r3):
    whole = jax.ShapeDtypeStruct((BLK, D), BF)
    return pl.pallas_call(
        add2_kernel,
        out_shape=(
            jax.ShapeDtypeStruct((BLK, D), F32),
            whole,
            whole,
            jax.ShapeDtypeStruct((CUT, D), BF),
            jax.ShapeDtypeStruct((BLK - CUT, D), BF),
        ),
        compiler_params=ask(12),
        name="add2",
        cost_estimate=pl.CostEstimate(flops=0, bytes_accessed=5 * MB, transcendentals=0),
    )(o0, r1, r3)


def add3_kernel(f1, ra, f3, rb, s1, s3):
    s1[:CUT] = (f1[:CUT].astype(F32) + ra[...].astype(F32)).astype(BF)
    s1[CUT:] = f1[CUT:]
    s3[:CUT] = f3[:CUT]
    s3[CUT:] = (f3[CUT:].astype(F32) + rb[...].astype(F32)).astype(BF)


def add3(f1, ra, f3, rb):
    out = jax.ShapeDtypeStruct((BLK, D), BF)
    return pl.pallas_call(
        add3_kernel,
        out_shape=(out, out),
        compiler_params=ask(12),
        name="add3",
        cost_estimate=pl.CostEstimate(flops=0, bytes_accessed=MB, transcendentals=0),
    )(f1, ra, f3, rb)


def last_kernel(a0, a1, a3, b0, b1, b3, gu_ref, dn_ref):
    for half, (f0, r1, r3) in enumerate(((a0, a1, a3), (b0, b1, b3))):
        total = f0[...] + r1[...].astype(F32) + r3[...].astype(F32)
        for e in range(2):
            j = 2 * half + e
            for a in range(4):
                for b in range(3):
                    n = a * 3 + b
                    top, left = 48 * e + 16 * (n // 4), 256 * (n % 4)
                    gu_ref[16 * a : 16 * a + 16, j, 256 * b : 256 * b + 256] = total[top : top + 16, left : left + 256]
            dn_ref[:, j, :] = total[96 + DN_ROWS * e : 96 + DN_ROWS * (e + 1), :]


def last(*pieces):
    return pl.pallas_call(
        last_kernel,
        out_shape=(
            jax.ShapeDtypeStruct((GU_ROWS, EXP, 2 * FF), F32),
            jax.ShapeDtypeStruct((DN_ROWS, EXP, D), F32),
        ),
        compiler_params=ask(12),
        name="last",
        cost_estimate=pl.CostEstimate(flops=0, bytes_accessed=4 * MB, transcendentals=0),
    )(*pieces)


def along(axis, step):
    pairs = []
    for i in range(SIDE * SIDE):
        x, y = divmod(i, SIDE)
        x, y = ((x + step) % SIDE, y) if axis == 0 else (x, (y + step) % SIDE)
        pairs.append((i, x * SIDE + y))
    return pairs


def move(block, axis, step):
    return lax.ppermute(block, "dp", along(axis, step))


def stage_one(axis, first, o0, o1, o3, o2a, o2b):
    ra, rb = move(o2a, axis, 1), move(o2b, axis, -1)
    ra, rb = after(ra, first), after(rb, first)
    s1, s3 = add1(o1, ra, o3, rb)
    r1, r3 = move(s1, axis, 1), move(s3, axis, -1)
    return list(add2(o0, r1, r3))


def stage_two(axis, f0, f1, f3, f2a, f2b):
    ra, rb = move(f2a, axis, 1), move(f2b, axis, -1)
    s1, s3 = add3(f1, ra, f3, rb)
    return f0, move(s1, axis, 1), move(s3, axis, -1)


def after(*blocks):
    return lax.optimization_barrier(blocks)[0]


def hop(block):
    pairs = []
    for i in range(OWN):
        z, core = divmod(i, 2)
        pairs.append((i, 2 * ((z + 1 - 2 * core) % LINE) + core))
    return lax.ppermute(block, "expert", pairs)


def swap(block):
    return lax.ppermute(block, "expert", [(i, i ^ 1) for i in range(OWN)])


def per_device(tokens, out_grad, expert_ids, gates, w_gate_up, w_down):
    me = jnp.stack([lax.axis_index("dp"), lax.axis_index("expert")]).astype(jnp.int32)
    own = prep(me, tokens, out_grad, expert_ids.T, gates.T)
    chunks, mine, got = [], [], []

    def run(pays):
        *chunk, keep = work(me, pays, w_gate_up, w_down)
        chunks.append(chunk[:4])
        mine.append(keep)
        got.extend(swap(give) for give in chunk[4:])

    near_by = pair(me, own, swap(own))
    came = hop(near_by)
    run((near_by,))
    came = after(came, mine[-1])
    for k in range(1, 4):
        pays = (came, swap(came))
        came = hop(came if k < 3 else part(me, came))
        run(pays)
        came = after(came, got[-1] if k < 3 else mine[-1])
    run((came, swap(came)))
    blocks_a = grads(0, me, chunks)
    blocks_b = grads(1, me, chunks)
    came = hop(far(mine[4], got[3]))
    first = near(me, mine[3], got[2], came)
    came = hop(first)
    for k in (2, 1):
        came = hop(near(me, mine[k], got[k - 1], came))
    keep, *give = home(me, mine[0], came)
    in_grad = done(keep, *[swap(half) for half in give])
    a, b = stage_one(0, first, *blocks_a), stage_one(1, first, *blocks_b)
    a[3], a[4] = after(a[3], b[3]), after(a[4], b[3])
    b[3], b[4] = after(b[3], a[3]), after(b[4], a[4])
    a, b = stage_two(1, *a), stage_two(0, *b)
    gu, dn = last(*a, *b)
    return in_grad, gu, dn


def solution(mesh):
    spec = P(("dp", "expert"), None)
    return jax.shard_map(
        per_device,
        mesh=mesh,
        in_specs=(spec, spec, spec, spec, P("expert", None, None), P("expert", None, None)),
        out_specs=(spec, P("dp", "expert", None), P("dp", "expert", None)),
        check_vma=False,
    )
```

```python
import functools

import jax
import jax.numpy as jnp
from jax import lax
from jax.experimental import pallas as pl
from jax.experimental.pallas import tpu as pltpu
from jax.sharding import PartitionSpec as P

TOK = 128
TOP = 8
D = 1024
FF = 384
CAP = 24
EXP = 4
OWN = 16
LINE = 8
SIDE = 4
GU_ROWS = D // 16
DN_ROWS = FF // 16
PAIR = 2 * CAP
ROWS = OWN * CAP
BLK = 2 * (3 * GU_ROWS // 4 + DN_ROWS)
CUT = 80
LANES = 128
PARTS = D // LANES
PAY = 2 * PARTS + 1
BF = jnp.bfloat16
F32 = jnp.float32
MB = 1 << 20


def dot(a, b, dims):
    return lax.dot_general(a, b, (dims, ((), ())), preferred_element_type=F32)


NN = ((1,), (0,))
NT = ((1,), (1,))
TN = ((0,), (0,))


def ask(limit):
    return pltpu.CompilerParams(vmem_limit_bytes=limit * MB)


def prep_kernel(me_ref, x_ref, g_ref, ids_ref, gates_ref, out_ref):
    for i in range(PARTS):
        out_ref[i] = x_ref[:, i * LANES : (i + 1) * LANES]
        out_ref[PARTS + i] = g_ref[:, i * LANES : (i + 1) * LANES]
    gate = gates_ref[...]
    high = gate.astype(BF)
    rest = gate - high.astype(F32)
    mid = rest.astype(BF)
    low = (rest - mid.astype(F32)).astype(BF)
    out_ref[2 * PARTS] = jnp.zeros((TOK, LANES), BF)
    out_ref[2 * PARTS, 0:16] = jnp.concatenate([ids_ref[...].astype(F32).astype(BF), high], axis=0)
    out_ref[2 * PARTS, 16:32] = jnp.concatenate([mid, low], axis=0)


def prep(me, tokens, out_grad, ids_t, gates_t):
    return pl.pallas_call(
        prep_kernel,
        out_shape=jax.ShapeDtypeStruct((PAY, TOK, LANES), BF),
        in_specs=[pl.BlockSpec(memory_space=pltpu.SMEM)] + [pl.BlockSpec(memory_space=pltpu.VMEM)] * 4,
        compiler_params=ask(58),
        name="prep",
        cost_estimate=pl.CostEstimate(flops=0, bytes_accessed=MB, transcendentals=0),
    )(me, tokens, out_grad, ids_t, gates_t)


def pair_kernel(me_ref, own_ref, other_ref, out_ref):
    core = me_ref[1] & 1
    out_ref[core] = own_ref[...]
    out_ref[1 - core] = other_ref[...]


def pair(me, own, other):
    return pl.pallas_call(
        pair_kernel,
        out_shape=jax.ShapeDtypeStruct((2, PAY, TOK, LANES), BF),
        in_specs=[pl.BlockSpec(memory_space=pltpu.SMEM)] + [pl.BlockSpec(memory_space=pltpu.VMEM)] * 2,
        compiler_params=ask(8),
        name="pair",
        cost_estimate=pl.CostEstimate(flops=0, bytes_accessed=2 * MB, transcendentals=0),
    )(me, own, other)


def part_kernel(me_ref, in_ref, out_ref):
    out_ref[...] = in_ref[:, pl.ds((me_ref[1] & 1) * PARTS, PARTS + 1)]


def part(me, block):
    return pl.pallas_call(
        part_kernel,
        out_shape=jax.ShapeDtypeStruct((2, PARTS + 1, TOK, LANES), BF),
        in_specs=[pl.BlockSpec(memory_space=pltpu.SMEM), pl.BlockSpec(memory_space=pltpu.VMEM)],
        compiler_params=ask(8),
        name="part",
        cost_estimate=pl.CostEstimate(flops=0, bytes_accessed=2 * MB, transcendentals=0),
    )(me, block)


def work_kernel(pairs, split, me_ref, *refs):
    count = 2 if split else pairs
    pays, refs = refs[:count], refs[count:]
    wgu_ref, wdn_ref, x_out, s_out, d_out, h_out = refs[:6]
    sums_out = refs[6:-4]
    xs, ss, rg, oh = refs[-4:]
    front = (me_ref[1] & 1) == 0
    j = pl.program_id(0)

    @pl.when(j == 0)
    def _():
        first = (me_ref[1] * EXP).astype(F32)
        before = (lax.broadcasted_iota(jnp.int32, (TOK, TOK), 0) < lax.broadcasted_iota(jnp.int32, (TOK, TOK), 1)).astype(BF)
        row = lax.broadcasted_iota(jnp.int32, (PAIR, 2 * TOK), 0).astype(F32)
        for n in range(pairs):
            if split:

                def take(core, i):
                    if i < PARTS:
                        return jnp.where(front, pays[0][core, i], pays[1][core, i])
                    return jnp.where(front, pays[1][core, i - PARTS], pays[0][core, i - PARTS])

            else:

                def take(core, i, ref=pays[n]):
                    return ref[core, i]

            x = jnp.concatenate([jnp.concatenate([take(core, i) for i in range(PARTS)], axis=1) for core in range(2)], axis=0)
            g = jnp.concatenate([jnp.concatenate([take(core, PARTS + i) for i in range(PARTS)], axis=1) for core in range(2)], axis=0)
            named, gate = [], []
            for core in range(2):
                meta = take(core, 2 * PARTS)[0:32].astype(F32)
                meta_a, meta_b = meta[0:16], meta[16:32]
                ids = meta_a[0:TOP]
                gates = (meta_a[TOP:] + meta_b[0:TOP]) + meta_b[TOP:]
                for e in range(EXP):
                    hit = ids == first + float(e)
                    named.append(jnp.sum(jnp.where(hit, 1.0, 0.0), axis=0, keepdims=True))
                    gate.append(jnp.sum(jnp.where(hit, gates, 0.0), axis=0, keepdims=True))
            mask = jnp.concatenate(named, axis=0)
            rank = dot(mask.astype(BF), before, NN)
            target = jnp.where(mask > 0.5, rank, -1000.0)
            picks, weights = [], []
            for e in range(EXP):
                place = jnp.concatenate([target[e : e + 1], target[EXP + e : EXP + e + 1] + float(CAP)], axis=1)
                gates = jnp.concatenate([gate[e], gate[EXP + e]], axis=1)
                hit = row == place
                picks.append(jnp.where(hit, 1.0, 0.0))
                weights.append(jnp.sum(jnp.where(hit, gates, 0.0), axis=1, keepdims=True))
            pick = jnp.concatenate(picks, axis=0).astype(BF)
            weight = jnp.concatenate(weights, axis=0)
            oh[n] = pick
            x_rows = dot(pick, x, NN).astype(BF)
            s_rows = (dot(pick, g, NN) * weight).astype(BF)
            for e in range(EXP):
                xs[e, n * PAIR : (n + 1) * PAIR] = x_rows[e * PAIR : (e + 1) * PAIR]
                ss[e, n * PAIR : (n + 1) * PAIR] = s_rows[e * PAIR : (e + 1) * PAIR]

    x, s = xs[j], ss[j]
    x_out[0] = x
    s_out[0] = s
    both = dot(x, wgu_ref[0], NN)
    gate_pre, up_val = both[:, :FF], both[:, FF:]
    sig = jax.nn.sigmoid(gate_pre)
    act = gate_pre * sig
    h_out[0] = (act * up_val).astype(BF)
    dh = dot(s, wdn_ref[0], NT)
    d_gate = dh * up_val * sig * (1.0 + gate_pre * (1.0 - sig))
    d_both = jnp.concatenate([d_gate, dh * act], axis=1).astype(BF)
    d_out[0] = d_both
    rg[j] = dot(d_both, wgu_ref[0], NT).astype(BF)

    @pl.when(j == EXP - 1)
    def _():
        for n in range(pairs):
            rows = jnp.concatenate([rg[e, n * PAIR : (n + 1) * PAIR, :] for e in range(EXP)], axis=0)
            sums = dot(oh[n], rows, TN).astype(BF)
            if split:
                sums_out[0][...] = jnp.where(front, sums[TOK:], sums[:TOK])
                sums_out[1][...] = jnp.where(front, sums[:TOK], sums[TOK:])
            else:
                sums_out[n][0] = sums[:TOK]
                sums_out[n][1] = sums[TOK:]


def work(me, pays, w_gate_up, w_down):
    split = pays[0].shape[1] != PAY
    pairs = 1 if split else len(pays)
    rows = pairs * PAIR
    widths = (D, D, 2 * FF, FF)

    def one(j, me):
        return (j, 0, 0)

    shape = (TOK, D) if split else (2, TOK, D)
    once = pl.Buffered(1)
    return pl.pallas_call(
        functools.partial(work_kernel, pairs, split),
        out_shape=tuple(jax.ShapeDtypeStruct((EXP, rows, width), BF) for width in widths)
        + (jax.ShapeDtypeStruct(shape, BF),) * len(pays),
        grid_spec=pltpu.PrefetchScalarGridSpec(
            num_scalar_prefetch=1,
            grid=(EXP,),
            in_specs=[pl.BlockSpec(pay.shape, lambda j, me: (0, 0, 0, 0), pipeline_mode=once) for pay in pays]
            + [pl.BlockSpec((1, D, 2 * FF), one), pl.BlockSpec((1, FF, D), one)],
            out_specs=tuple(pl.BlockSpec((1, rows, width), one) for width in widths)
            + (pl.BlockSpec(shape, lambda j, me: (0,) * len(shape)),) * len(pays),
            scratch_shapes=[
                pltpu.VMEM((EXP, rows, D), BF),
                pltpu.VMEM((EXP, rows, D), BF),
                pltpu.VMEM((EXP, rows, D), BF),
                pltpu.VMEM((pairs, EXP * PAIR, 2 * TOK), BF),
            ],
        ),
        compiler_params=ask(20),
        name="work",
        cost_estimate=pl.CostEstimate(flops=2 * EXP * 256 * D * FF * 8, bytes_accessed=14 * MB, transcendentals=0),
    )(me, *pays, w_gate_up, w_down)


def grads_kernel(parts, half, me_ref, *refs):
    chunks, (o0, o1, o3, o2a, o2b, xa, sa, da, ha, pgu, pdn) = refs[: 4 * len(parts)], refs[4 * len(parts) :]
    jj = pl.program_id(0)
    px, py = me_ref[0] >> 2, me_ref[0] & 3
    low = 0
    for c, rows in enumerate(parts):
        for ref, to in zip(chunks[4 * c : 4 * c + 4], (xa, sa, da, ha)):
            to[low : low + rows] = ref[0]
        low += rows
    pgu[...] = dot(xa[...], da[...], TN)
    pdn[jj] = dot(ha[...], sa[...], TN)

    def outs():
        for first in range(SIDE):
            for second in range(SIDE):
                if first == 2:
                    ref, at = (o2a, second) if second < 2 else (o2b, second - 2)
                else:
                    ref, at = {0: o0, 1: o1, 3: o3}[first], second
                dx, dy = (first, second) if half == 0 else (second, first)
                yield ((px + dx) & 3) * SIDE + ((py + dy) & 3), ref, at

    for step in range(2):

        @pl.when(jj == step)
        def _():
            for number, ref, at in outs():
                base = pl.multiple_of(number * GU_ROWS, GU_ROWS)
                for a in range(4):
                    for b in range(3):
                        n = a * 3 + b
                        top, left = 48 * step + 16 * (n // 4), 256 * (n % 4)
                        ref[at, top : top + 16, left : left + 256] = pgu[pl.ds(base + 16 * a, 16), 256 * b : 256 * b + 256].astype(BF)
                if step == 1:
                    low = pl.multiple_of(number * DN_ROWS, DN_ROWS)
                    ref[at, 96:BLK, :] = jnp.concatenate([pdn[0, pl.ds(low, DN_ROWS), :], pdn[1, pl.ds(low, DN_ROWS), :]], axis=0).astype(BF)


def grads(half, me, chunks):
    parts = tuple(chunk[0].shape[1] for chunk in chunks)
    widths = (D, D, 2 * FF, FF)

    def at(j, w):
        return (2 * half + j, 0, 0)

    def whole(j, w):
        return (0, 0, 0)

    counts = (4, 4, 4, 2, 2)
    return pl.pallas_call(
        functools.partial(grads_kernel, parts, half),
        out_shape=tuple(jax.ShapeDtypeStruct((n, BLK, D), BF) for n in counts),
        grid_spec=pltpu.PrefetchScalarGridSpec(
            num_scalar_prefetch=1,
            grid=(2,),
            in_specs=[pl.BlockSpec((1, rows, width), at) for rows in parts for width in widths],
            out_specs=tuple(pl.BlockSpec((n, BLK, D), whole) for n in counts),
            scratch_shapes=[pltpu.VMEM((ROWS, width), BF) for width in widths] + [pltpu.VMEM((D, 2 * FF), F32), pltpu.VMEM((2, FF, D), F32)],
        ),
        compiler_params=ask(26),
        name="grads",
        cost_estimate=pl.CostEstimate(flops=2 * 2 * ROWS * D * FF * 3, bytes_accessed=12 * MB, transcendentals=0),
    )(me, *[a for chunk in chunks for a in chunk])


def far_kernel(mine_ref, got_ref, out_ref):
    out_ref[...] = (mine_ref[...].astype(F32) + got_ref[...].astype(F32)).astype(BF)


def far(mine, got):
    return pl.pallas_call(
        far_kernel,
        out_shape=jax.ShapeDtypeStruct((TOK, D), BF),
        compiler_params=ask(8),
        name="far",
        cost_estimate=pl.CostEstimate(flops=0, bytes_accessed=MB, transcendentals=0),
    )(mine, got)


def near_kernel(me_ref, mine_ref, got_ref, came_ref, out_ref):
    if len(came_ref.shape) == 3:
        out_ref[...] = ((mine_ref[...].astype(F32) + got_ref[...].astype(F32)) + came_ref[...].astype(F32)).astype(BF)
    else:
        core = me_ref[1] & 1
        out_ref[core] = ((mine_ref[core].astype(F32) + got_ref[core].astype(F32)) + came_ref[...].astype(F32)).astype(BF)
        out_ref[1 - core] = (mine_ref[1 - core].astype(F32) + got_ref[1 - core].astype(F32)).astype(BF)


def near(me, mine, got, came):
    return pl.pallas_call(
        near_kernel,
        out_shape=jax.ShapeDtypeStruct((2, TOK, D), BF),
        in_specs=[pl.BlockSpec(memory_space=pltpu.SMEM)] + [pl.BlockSpec(memory_space=pltpu.VMEM)] * 3,
        compiler_params=ask(8),
        name="near",
        cost_estimate=pl.CostEstimate(flops=0, bytes_accessed=2 * MB, transcendentals=0),
    )(me, mine, got, came)


def home_kernel(me_ref, mine_ref, came_ref, keep_ref, give_a, give_b):
    core = me_ref[1] & 1
    keep_ref[...] = mine_ref[core].astype(F32) + came_ref[core].astype(F32)
    give = (mine_ref[1 - core].astype(F32) + came_ref[1 - core].astype(F32)).astype(BF)
    give_a[...] = give[: TOK // 2]
    give_b[...] = give[TOK // 2 :]


def home(me, mine, came):
    return pl.pallas_call(
        home_kernel,
        out_shape=(jax.ShapeDtypeStruct((TOK, D), F32),) + (jax.ShapeDtypeStruct((TOK // 2, D), BF),) * 2,
        in_specs=[pl.BlockSpec(memory_space=pltpu.SMEM)] + [pl.BlockSpec(memory_space=pltpu.VMEM)] * 2,
        compiler_params=ask(8),
        name="home",
        cost_estimate=pl.CostEstimate(flops=0, bytes_accessed=MB, transcendentals=0),
    )(me, mine, came)


def done_kernel(mine_ref, a_ref, b_ref, out_ref):
    half = TOK // 2
    out_ref[:half] = (mine_ref[:half] + a_ref[...].astype(F32)).astype(BF)
    out_ref[half:] = (mine_ref[half:] + b_ref[...].astype(F32)).astype(BF)


def done(mine, a, b):
    return pl.pallas_call(
        done_kernel,
        out_shape=jax.ShapeDtypeStruct((TOK, D), BF),
        compiler_params=ask(8),
        name="done",
        cost_estimate=pl.CostEstimate(flops=0, bytes_accessed=MB, transcendentals=0),
    )(mine, a, b)


def add1_kernel(o1, ra, o3, rb, s1, s3):
    s1[0:2] = (o1[0:2].astype(F32) + ra[...].astype(F32)).astype(BF)
    s1[2:4] = o1[2:4]
    s3[0:2] = o3[0:2]
    s3[2:4] = (o3[2:4].astype(F32) + rb[...].astype(F32)).astype(BF)


def add1(o1, ra, o3, rb):
    out = jax.ShapeDtypeStruct((SIDE, BLK, D), BF)
    return pl.pallas_call(
        add1_kernel,
        out_shape=(out, out),
        compiler_params=ask(12),
        name="add1",
        cost_estimate=pl.CostEstimate(flops=0, bytes_accessed=6 * MB, transcendentals=0),
    )(o1, ra, o3, rb)


def add2_kernel(o0, r1, r3, f0, f1, f3, f2a, f2b):
    def total(k):
        return (o0[k].astype(F32) + r1[k].astype(F32)) + r3[k].astype(F32)

    f0[...] = total(0)
    f1[...] = total(1).astype(BF)
    f3[...] = total(3).astype(BF)
    two = total(2).astype(BF)
    f2a[...] = two[:CUT]
    f2b[...] = two[CUT:]


def add2(o0, r1, r3):
    whole = jax.ShapeDtypeStruct((BLK, D), BF)
    return pl.pallas_call(
        add2_kernel,
        out_shape=(
            jax.ShapeDtypeStruct((BLK, D), F32),
            whole,
            whole,
            jax.ShapeDtypeStruct((CUT, D), BF),
            jax.ShapeDtypeStruct((BLK - CUT, D), BF),
        ),
        compiler_params=ask(12),
        name="add2",
        cost_estimate=pl.CostEstimate(flops=0, bytes_accessed=5 * MB, transcendentals=0),
    )(o0, r1, r3)


def add3_kernel(f1, ra, f3, rb, s1, s3):
    s1[:CUT] = (f1[:CUT].astype(F32) + ra[...].astype(F32)).astype(BF)
    s1[CUT:] = f1[CUT:]
    s3[:CUT] = f3[:CUT]
    s3[CUT:] = (f3[CUT:].astype(F32) + rb[...].astype(F32)).astype(BF)


def add3(f1, ra, f3, rb):
    out = jax.ShapeDtypeStruct((BLK, D), BF)
    return pl.pallas_call(
        add3_kernel,
        out_shape=(out, out),
        compiler_params=ask(12),
        name="add3",
        cost_estimate=pl.CostEstimate(flops=0, bytes_accessed=MB, transcendentals=0),
    )(f1, ra, f3, rb)


def last_kernel(a0, a1, a3, b0, b1, b3, gu_ref, dn_ref):
    for half, (f0, r1, r3) in enumerate(((a0, a1, a3), (b0, b1, b3))):
        total = f0[...] + r1[...].astype(F32) + r3[...].astype(F32)
        for e in range(2):
            j = 2 * half + e
            for a in range(4):
                for b in range(3):
                    n = a * 3 + b
                    top, left = 48 * e + 16 * (n // 4), 256 * (n % 4)
                    gu_ref[16 * a : 16 * a + 16, j, 256 * b : 256 * b + 256] = total[top : top + 16, left : left + 256]
            dn_ref[:, j, :] = total[96 + DN_ROWS * e : 96 + DN_ROWS * (e + 1), :]


def last(*pieces):
    return pl.pallas_call(
        last_kernel,
        out_shape=(
            jax.ShapeDtypeStruct((GU_ROWS, EXP, 2 * FF), F32),
            jax.ShapeDtypeStruct((DN_ROWS, EXP, D), F32),
        ),
        compiler_params=ask(12),
        name="last",
        cost_estimate=pl.CostEstimate(flops=0, bytes_accessed=4 * MB, transcendentals=0),
    )(*pieces)


def along(axis, step):
    pairs = []
    for i in range(SIDE * SIDE):
        x, y = divmod(i, SIDE)
        x, y = ((x + step) % SIDE, y) if axis == 0 else (x, (y + step) % SIDE)
        pairs.append((i, x * SIDE + y))
    return pairs


def move(block, axis, step):
    return lax.ppermute(block, "dp", along(axis, step))


def stage_one(axis, first, o0, o1, o3, o2a, o2b):
    ra, rb = move(o2a, axis, 1), move(o2b, axis, -1)
    ra, rb = after(ra, first), after(rb, first)
    s1, s3 = add1(o1, ra, o3, rb)
    r1, r3 = move(s1, axis, 1), move(s3, axis, -1)
    return list(add2(o0, r1, r3))


def stage_two(axis, f0, f1, f3, f2a, f2b):
    ra, rb = move(f2a, axis, 1), move(f2b, axis, -1)
    s1, s3 = add3(f1, ra, f3, rb)
    return f0, move(s1, axis, 1), move(s3, axis, -1)


def after(*blocks):
    return lax.optimization_barrier(blocks)[0]


def hop(block):
    pairs = []
    for i in range(OWN):
        z, core = divmod(i, 2)
        pairs.append((i, 2 * ((z + 1 - 2 * core) % LINE) + core))
    return lax.ppermute(block, "expert", pairs)


def swap(block):
    return lax.ppermute(block, "expert", [(i, i ^ 1) for i in range(OWN)])


def per_device(tokens, out_grad, expert_ids, gates, w_gate_up, w_down):
    me = jnp.stack([lax.axis_index("dp"), lax.axis_index("expert")]).astype(jnp.int32)
    own = prep(me, tokens, out_grad, expert_ids.T, gates.T)
    chunks, mine, got = [], [], []

    def run(pays):
        *chunk, give, keep = work(me, pays, w_gate_up, w_down)
        chunks.append(chunk[:4])
        mine.extend([*chunk[4:], keep])
        got.append(swap(give))

    near_by = pair(me, own, swap(own))
    came = hop(near_by)
    for k in range(1, 4):
        pays = (came, swap(came))
        came = hop(came if k < 3 else part(me, came))
        run((near_by, *pays) if k == 1 else pays)
        came = after(came, got[-1] if k < 3 else mine[-1])
    run((came, swap(came)))
    blocks_a = grads(0, me, chunks)
    blocks_b = grads(1, me, chunks)
    came = hop(far(mine[4], got[3]))
    first = near(me, mine[3], got[2], came)
    came = hop(first)
    for k in (2, 1):
        came = hop(near(me, mine[k], got[k - 1], came))
    keep, *give = home(me, mine[0], came)
    in_grad = done(keep, *[swap(half) for half in give])
    a, b = stage_one(0, first, *blocks_a), stage_one(1, first, *blocks_b)
    b[3], b[4] = after(b[3], a[3]), after(b[4], a[4])
    a, b = stage_two(1, *a), stage_two(0, *b)
    gu, dn = last(*a, *b)
    return in_grad, gu, dn


def solution(mesh):
    spec = P(("dp", "expert"), None)
    return jax.shard_map(
        per_device,
        mesh=mesh,
        in_specs=(spec, spec, spec, spec, P("expert", None, None), P("expert", None, None)),
        out_specs=(spec, P("dp", "expert", None), P("dp", "expert", None)),
        check_vma=False,
    )
```
